128 devices in a mesh: section: 8 (over x, core), dp: 16 (over z, y).
Axes of the slice: x: 4, y: 4, z: 4, core: 2. Of those that a mesh axis runs over, the one named last changes fastest.
Arguments:
- text: bfloat16 [16, 128, 8192], P('dp'), may hold values from -6 to 6
- cotangent: bfloat16 [16, 128, 8192], P('dp'), may hold values from -6 to 6
- dec_down: bfloat16 [8, 8192, 128], P('section'), may hold values from -0.0625 to 0.0625
- dec_up: bfloat16 [8, 128, 8192], P('section'), may hold values from -0.5 to 0.5
- images: bfloat16 [16, 8, 2, 32, 3200], P('dp', 'section'), may hold values from -6 to 6
- enc_down: bfloat16 [3200, 128], replicated, may hold values from -0.109375 to 0.109375
- enc_up: bfloat16 [128, 3200], replicated, may hold values from -0.5 to 0.5
- proj_in: bfloat16 [12800, 128], replicated, may hold values from -0.0546875 to 0.0546875
- proj_out: bfloat16 [128, 8192], replicated, may hold values from -0.5 to 0.5
- frame: int32 [16, 16], P('dp'), may hold values from -1 to 15, as said below
Outputs:
- grad_dec_down: float32 [8, 8192, 128], P('section', 'dp')
- grad_dec_up: float32 [8, 128, 8192], P('section', None, 'dp')
- grad_enc_down: float32 [3200, 128], P(('section', 'dp'))
- grad_enc_up: float32 [128, 3200], P(None, ('section', 'dp'))
- grad_proj_in: float32 [12800, 128], P(('section', 'dp'))
- grad_proj_out: float32 [128, 8192], P(None, ('section', 'dp'))
The draws below stay inside these ranges and needn't reach their ends.
Inputs may be any that keep to these rules, and one draw needn't show every extreme that they name: In each row the entries that are not -1 are distinct; the largest frame and -1 occur in every draw.
All inputs are finite; a program needn't handle non-finite values.
Results may differ from the reference program's by a relative error of at most 0.035.
Values may be sent and summed in bfloat16 or wider, within the bound.
No kernel may reach another device: no remote copies, remote signals or barrier semaphores. Data moves between devices by JAX's collectives and lax.ppermute only.
A program may use at most 128 MiB of HBM per device.

```python
import jax
import jax.numpy as jnp
from jax import lax

D = 8192
E = 3200
RD = 128
RE = 128
RP = 128
PATCH = 32
SLOTS = 2
IMGTOK = 8
ROWS = 128
FRAMES = 16
SLOTS_ALL = 16
N_SECTION = 8
N_DP = 16


def draw_frame(key, part):
    key = jax.random.fold_in(key, 17)
    order_key, live_key = jax.random.split(key, 2)

    def one_group(group_key):
        first_key, second_key = jax.random.split(group_key)
        order = jax.random.permutation(first_key, FRAMES).astype(jnp.int32)
        top_place = jnp.argmax(order == FRAMES - 1)
        leading = order[0]
        order = order.at[top_place].set(leading).at[0].set(FRAMES - 1)
        chosen = order[:SLOTS_ALL]
        shuffle = jax.random.permutation(second_key, SLOTS_ALL)
        return (chosen[shuffle], order[1])
    values, dropped = jax.vmap(one_group)(jax.random.split(order_key, N_DP))
    alive = jax.random.randint(live_key, (N_DP, SLOTS_ALL), 0, 2) == 1
    alive = (alive | (values == FRAMES - 1)) & (values != dropped[:, None])
    return jnp.where(alive, values, -1).astype(jnp.int32)


def steps_of(key, extent, shards, least, top_value):
    loudness, own = 1.0, jax.random.fold_in(key, 6)
    for axis_at, blocks in shards:
        heights = jnp.exp(jax.random.uniform(jax.random.fold_in(own, axis_at), (blocks,), jnp.float32, least / len(shards), top_value / len(shards)))
        loudness = loudness * jnp.repeat(heights, extent[axis_at] // blocks).reshape([-1 if axis == axis_at else 1 for axis in range(len(extent))])
    return loudness


def noise(rng, shape, deviation, limit, shards=(), kind=jnp.bfloat16):
    level = steps_of(rng, shape, shards, -0.22, 0.18) if shards else 1.0
    result = jax.random.normal(rng, shape, jnp.float32) * deviation * level
    return jnp.minimum(jnp.maximum(result, -limit), limit).astype(kind)


def setup_inputs(seed: int = 0) -> dict:
    arg_keys = jax.random.split(jax.random.key(seed), 11)
    text = noise(arg_keys[0], (N_DP, ROWS, D), 1.0, 6.0, ((0, 16),))
    cotangent = noise(arg_keys[1], (N_DP, ROWS, D), 1.0, 6.0, ((0, 16),))
    dec_down = noise(arg_keys[2], (N_SECTION, D, RD), D ** -0.5, 0.0625, ((0, 8),))
    dec_up = noise(arg_keys[3], (N_SECTION, RD, D), RD ** -0.5, 0.5, ((0, 8),))
    images = noise(arg_keys[4], (N_DP, N_SECTION, SLOTS, PATCH, E), 1.0, 6.0, ((0, 16), (1, 8)))
    enc_down = noise(arg_keys[5], (E, RE), E ** -0.5, 0.109375)
    enc_up = noise(arg_keys[6], (RE, E), RE ** -0.5, 0.5)
    proj_in = noise(arg_keys[7], (4 * E, RP), (4 * E) ** -0.5, 0.0546875)
    proj_out = noise(arg_keys[8], (RP, D), RP ** -0.5, 0.5)
    frame = draw_frame(jax.random.fold_in(arg_keys[10], 71), 0)
    return {"text": text, "cotangent": cotangent, "dec_down": dec_down, "dec_up": dec_up, "images": images, "enc_down": enc_down, "enc_up": enc_up, "proj_in": proj_in, "proj_out": proj_out, "frame": frame}


EPS = 1e-06
GELU_C = 0.7978845608028654

def gelu_tanh(value):
    return 0.5 * value * (1.0 + jnp.tanh(GELU_C * (value + 0.044715 * value * value * value)))

def gelu_slope(value):
    inner = jnp.tanh(GELU_C * (value + 0.044715 * value * value * value))
    return 0.5 * (1.0 + inner) + 0.5 * value * (1.0 - inner * inner) * GELU_C * (1.0 + 3.0 * 0.044715 * value * value)

def silu_slope(value):
    sig = jax.nn.sigmoid(value)
    return sig * (1.0 + value * (1.0 - sig))

def norm_scale(rows32):
    return lax.rsqrt(lax.optimization_barrier(jnp.mean(rows32 * rows32, axis=-1, keepdims=True)) + EPS)

def norm_back(rows32, scale, grad):
    normed = rows32 * scale
    return scale * (grad - normed * lax.optimization_barrier(jnp.mean(grad * normed, axis=-1, keepdims=True)))

def fmul(form, left, right):
    return jnp.einsum(form, left.astype(jnp.float32), right.astype(jnp.float32))

def reference(text, cotangent, dec_down, dec_up, images, enc_down, enc_up, proj_in, proj_out, frame):
    count = N_DP * N_SECTION * SLOTS
    patches = images.reshape(count, PATCH, E)
    patch32 = patches.astype(jnp.float32)
    enc_scale = norm_scale(patch32)
    enc_normed = (patch32 * enc_scale).astype(jnp.bfloat16)
    enc_pre = fmul('bpe,er->bpr', enc_normed, enc_down)
    enc_act = gelu_tanh(enc_pre).astype(jnp.bfloat16)
    enc_out = (patch32 + fmul('bpr,re->bpe', enc_act, enc_up)).astype(jnp.bfloat16)
    merged = enc_out.reshape(count, IMGTOK, 4 * E).astype(jnp.float32)
    proj_scale = norm_scale(merged)
    proj_normed = (merged * proj_scale).astype(jnp.bfloat16)
    proj_pre = fmul('bic,cr->bir', proj_normed, proj_in)
    proj_act = gelu_tanh(proj_pre).astype(jnp.bfloat16)
    image_rows = fmul('bir,rd->bid', proj_act, proj_out).astype(jnp.bfloat16)
    slot_rows = image_rows.reshape(N_DP, SLOTS_ALL, IMGTOK, D)
    match = (frame[:, None, :] == jnp.arange(FRAMES, dtype=jnp.int32)[None, :, None]).astype(jnp.float32)
    placed = jnp.einsum('rfk,rkid->rfid', match, slot_rows.astype(jnp.float32))
    live = (lax.optimization_barrier(jnp.sum(match, axis=-1)) > 0.5)[:, :, None, None]
    base = text.reshape(N_DP, FRAMES, IMGTOK, D).astype(jnp.float32)
    hidden = jnp.where(live, placed, base).astype(jnp.bfloat16).reshape(N_DP * ROWS, D)
    stored = []
    for layer in range(N_SECTION):
        stored.append(hidden)
        h32 = hidden.astype(jnp.float32)
        normed = (h32 * norm_scale(h32)).astype(jnp.bfloat16)
        pre = jnp.dot(normed, dec_down[layer], preferred_element_type=jnp.float32)
        act = jax.nn.silu(pre).astype(jnp.bfloat16)
        hidden = (h32 + jnp.dot(act, dec_up[layer], preferred_element_type=jnp.float32)).astype(jnp.bfloat16)
    grad = cotangent.reshape(N_DP * ROWS, D)
    down_list = []
    up_list = []
    for layer in reversed(range(N_SECTION)):
        h32 = stored[layer].astype(jnp.float32)
        scale = norm_scale(h32)
        normed = (h32 * scale).astype(jnp.bfloat16)
        pre = jnp.dot(normed, dec_down[layer], preferred_element_type=jnp.float32)
        act = jax.nn.silu(pre).astype(jnp.bfloat16)
        d_act = jnp.dot(grad, dec_up[layer].T, preferred_element_type=jnp.float32)
        d_pre = (d_act * silu_slope(pre)).astype(jnp.bfloat16)
        d_normed = jnp.dot(d_pre, dec_down[layer].T, preferred_element_type=jnp.float32)
        part_down = fmul('rtd,rtk->rdk', normed.reshape(N_DP, ROWS, D), d_pre.reshape(N_DP, ROWS, RD))
        part_up = fmul('rtk,rtd->rkd', act.reshape(N_DP, ROWS, RD), grad.reshape(N_DP, ROWS, D))
        down_list.append(lax.optimization_barrier(jnp.sum(part_down.astype(jnp.bfloat16).astype(jnp.float32), axis=0)))
        up_list.append(lax.optimization_barrier(jnp.sum(part_up.astype(jnp.bfloat16).astype(jnp.float32), axis=0)))
        grad = (grad.astype(jnp.float32) + norm_back(h32, scale, d_normed)).astype(jnp.bfloat16)
    grad_dec_down = jnp.stack(down_list[::-1])
    grad_dec_up = jnp.stack(up_list[::-1])
    first_grad = grad.reshape(N_DP, FRAMES, IMGTOK, D).astype(jnp.float32)
    image_grad = jnp.einsum('rfk,rfid->rkid', match, first_grad).astype(jnp.bfloat16).reshape(count, IMGTOK, D)
    grad_proj_out = fmul('bir,bid->rd', proj_act, image_grad)
    d_proj = (fmul('bid,rd->bir', image_grad, proj_out) * gelu_slope(proj_pre)).astype(jnp.bfloat16)
    grad_proj_in = fmul('bic,bir->cr', proj_normed, d_proj)
    d_pn = fmul('bir,cr->bic', d_proj, proj_in)
    d_merged = norm_back(merged, proj_scale, d_pn).reshape(count, PATCH, E).astype(jnp.bfloat16)
    grad_enc_up = fmul('bpr,bpe->re', enc_act, d_merged)
    d_enc = (fmul('bpe,re->bpr', d_merged, enc_up) * gelu_slope(enc_pre)).astype(jnp.bfloat16)
    grad_enc_down = fmul('bpe,bpr->er', enc_normed, d_enc)
    return (grad_dec_down, grad_dec_up, grad_enc_down, grad_enc_up, grad_proj_in, grad_proj_out)
```

```python
import functools

import jax
import jax.numpy as jnp
from jax import lax
from jax.experimental import pallas as pl
from jax.experimental.pallas import tpu as pltpu
from jax.sharding import PartitionSpec as P

EPS = 1e-06
GELU_C = 0.7978845608028654
BF = jnp.bfloat16
F32 = jnp.float32


def gelu_tanh(value):
    return 0.5 * value * (1.0 + jnp.tanh(GELU_C * (value + 0.044715 * value * value * value)))


def gelu_slope(value):
    inner = jnp.tanh(GELU_C * (value + 0.044715 * value * value * value))
    return 0.5 * (1.0 + inner) + 0.5 * value * (1.0 - inner * inner) * GELU_C * (
        1.0 + 3.0 * 0.044715 * value * value
    )


def norm_scale(rows32):
    return lax.rsqrt(jnp.mean(rows32 * rows32, axis=-1, keepdims=True) + EPS)


def dot(left, right, dims):
    return lax.dot_general(left, right, ((dims[:1], dims[1:]), ((), ())), preferred_element_type=F32)


def dot_nn(left, right):
    return dot(left, right, (1, 0))


def dot_tn(left, right):
    return dot(left, right, (0, 0))


def dot_nt(left, right):
    return dot(left, right, (1, 1))


def rank_kernel(
    layers, groups, width,
    place_ref, gram_ref, gath_ref, cot_ref, norm_ref, image_gram_ref, sel_ref,
    coef_ref, factor_ref, image_ref,
    weight, acts, act_cat, grads, scaled, back, pre_ref, slope_ref, inner_ref, scale_ref,
):
    rank = 128
    own = place_ref[0]

    def lay(layer, carry):
        for j in range(layers + 1):
            tile = gram_ref[pl.ds(layer * groups, groups), j * 16:(j + 1) * 16, :].astype(F32)
            rows = slice(j * rank, (j + 1) * rank)
            weight[layer, rows, :rank] = tile[:, :8, :].reshape(rank, rank).astype(BF)
            weight[layer, rows, rank:] = tile[:, 8:, :].reshape(rank, rank).astype(BF)
        return carry

    lax.fori_loop(0, layers, lay, 0)

    proj_pre = jnp.concatenate(
        [gath_ref[l, 4 * rank:4 * rank + 16, :] for l in range(layers)], axis=0
    ).astype(F32)
    sel = sel_ref[...]
    placed = dot_nn(sel, gelu_tanh(proj_pre).astype(BF))
    placed_half = placed.astype(BF)
    acts[0] = placed_half
    act_cat[:, :rank] = placed_half
    image_inner = dot_nn(placed_half, image_gram_ref[...])
    total = norm_ref[...] + jnp.sum(placed * image_inner, axis=1, keepdims=True)
    for l in range(layers):
        here = (l + 1) * rank
        scale = lax.rsqrt(jnp.maximum(total, 0.0) * (1.0 / width) + EPS)
        both = dot_nn(act_cat[:, :here], weight[l, :here, :])
        pre = scale * (gath_ref[l, :rank, :].astype(F32) + both[:, :rank])
        inner = gath_ref[l, rank:2 * rank, :].astype(F32) + both[:, rank:]
        sig = jax.nn.sigmoid(pre)
        act = (pre * sig).astype(BF)
        acts[l + 1] = act
        act_cat[:, here:here + rank] = act
        after = inner + dot_nn(act, weight[l, here:here + rank, rank:])
        total = total + jnp.sum(act.astype(F32) * (inner + after), axis=1, keepdims=True)
        pre_ref[l] = pre
        slope_ref[l] = sig * (1.0 + pre * (1.0 - sig))
        inner_ref[l] = after
        scale_ref[l] = scale
    back[...] = jnp.zeros_like(back)
    sums = jnp.zeros_like(total)
    for l in reversed(range(layers)):
        here = (l + 1) * rank
        cot = gath_ref[l, 2 * rank:3 * rank, :].astype(F32)
        d_act = cot - sums * inner_ref[l] + back[:, here:here + rank]
        d_pre = (d_act * slope_ref[l]).astype(BF).astype(F32)
        scale = scale_ref[l]
        mean = jnp.sum(d_pre * pre_ref[l], axis=1, keepdims=True) * (1.0 / width)
        grad = (scale * d_pre).astype(BF)
        part = (sums * acts[l + 1].astype(F32)).astype(BF)
        grads[l] = grad
        scaled[l + 1] = part
        pair = jnp.concatenate([grad, -part], axis=1)
        back[:, :here] += dot_nt(pair, weight[l, :here, :])
        sums = sums + scale * scale * mean
    d_image = cot_ref[...] - sums * image_inner + back[:, :rank]
    scaled[0] = (sums * placed).astype(BF)
    d_slot = dot_tn(sel, d_image.astype(BF))
    image_ref[0] = (d_slot * gelu_slope(proj_pre)).astype(BF)
    image_ref[1] = placed_half
    image_ref[2] = scaled[0]

    own_act = acts[own + 1]
    own_grad = grads[own]
    own_scaled = scaled[own + 1]
    factor_ref[0] = own_grad
    factor_ref[1] = own_act
    factor_ref[2] = own_scaled
    coef_ref[0] = dot_tn(acts[0], own_grad).astype(BF)
    for l in range(layers):
        low = l < own
        left = jnp.where(low, acts[l + 1], grads[l])
        right = jnp.where(low, own_grad, own_act)
        coef_ref[l + 1] = dot_tn(left, right).astype(BF)
    for l in range(layers + 1):
        low = l <= own + 1
        left = jnp.where(low, acts[l], scaled[l])
        right = jnp.where(low, own_scaled, own_act)
        coef_ref[layers + 1 + l] = dot_tn(left, right).astype(BF)


def rank_space(position, gram, gath, cot, norms, image_gram, sel, width):
    layers = gath.shape[0]
    groups = gram.shape[0] // layers
    rank = 128
    vmem = pl.BlockSpec(memory_space=pltpu.VMEM)
    tall = (layers + 1) * rank
    return pl.pallas_call(
        functools.partial(rank_kernel, layers, groups, width),
        in_specs=[pl.BlockSpec(memory_space=pltpu.SMEM)] + [vmem] * 6,
        out_specs=[vmem] * 3,
        out_shape=[
            jax.ShapeDtypeStruct((2 * layers + 2, rank, rank), BF),
            jax.ShapeDtypeStruct((3, rank, rank), BF),
            jax.ShapeDtypeStruct((3, rank, rank), BF),
        ],
        scratch_shapes=[
            pltpu.VMEM((layers, tall, 2 * rank), BF),
            pltpu.VMEM((layers + 1, rank, rank), BF),
            pltpu.VMEM((rank, tall), BF),
            pltpu.VMEM((layers, rank, rank), BF),
            pltpu.VMEM((layers + 1, rank, rank), BF),
            pltpu.VMEM((rank, tall), F32),
            pltpu.VMEM((layers, rank, rank), F32),
            pltpu.VMEM((layers, rank, rank), F32),
            pltpu.VMEM((layers, rank, rank), F32),
            pltpu.VMEM((layers, rank, 1), F32),
        ],
        compiler_params=pltpu.CompilerParams(vmem_limit_bytes=40 * 1024 * 1024),
    )(position.reshape(1).astype(jnp.int32), gram, gath, cot, norms, image_gram, sel)


def section_gather(value):
    count = lax.axis_size("section")
    parts = [value]
    for step in range(1, count):
        pairs = [((at + step) % count, at) for at in range(count)]
        parts.append(lax.ppermute(value, "section", pairs))
    return jnp.roll(jnp.stack(parts), lax.axis_index("section"), axis=0)


def split_pair(value):
    high = value.astype(BF)
    return high, (value - high.astype(F32)).astype(BF)


def shards(text, cotangent, dec_down, dec_up, images, enc_down, enc_up, proj_in, proj_out, frame):
    sections = lax.axis_size("section")
    groups = lax.axis_size("dp")
    sec = lax.axis_index("section")
    grp = lax.axis_index("dp")
    slot_count, patch_count, enc_width = images.shape[2:]
    tokens = patch_count // 4
    rows_total, width = text.shape[1:]
    rank = dec_down.shape[2]
    frame_total = rows_total // tokens
    weight_down = dec_down[0]
    weight_up = dec_up[0]
    frames = frame[0]
    text = text[0]
    cot = cotangent[0]
    piece = rank // groups

    own_rows = lax.dynamic_slice_in_dim(weight_up, grp * piece, piece, 0)
    up_rows = lax.all_gather(own_rows, "section", axis=0)

    slot_row = jnp.repeat(frames, tokens)[None, :]
    row = jnp.arange(rows_total, dtype=jnp.int32)[:, None]
    column = jnp.arange(rows_total, dtype=jnp.int32)[None, :]
    sel = (slot_row == row // tokens) & (row % tokens == column % tokens)
    live = jnp.any(sel, axis=1, keepdims=True)
    sel = sel.astype(BF)
    text = jnp.where(live, jnp.zeros_like(text), text)
    text_down = dot_nn(text, weight_down).astype(BF)
    text_up = dot_nt(text, weight_up).astype(BF)
    cot_up = dot_nt(cot, weight_up).astype(BF)
    cot_image = dot_nt(cot, proj_out)
    text32 = text.astype(F32)
    text_norm = jnp.sum(text32 * text32, axis=1, keepdims=True)
    image_gram = dot_nt(proj_out, proj_out).astype(BF)

    patches = images[0, 0].reshape(slot_count * patch_count, enc_width)
    patch32 = patches.astype(F32)
    enc_scale = norm_scale(patch32)
    enc_pre = dot_nn((patch32 * enc_scale).astype(BF), enc_down)
    enc_act = gelu_tanh(enc_pre).astype(BF)
    enc_out = (patch32 + dot_nn(enc_act, enc_up)).astype(BF)
    enc_inner = dot_nt(enc_out, enc_up)
    merged = enc_out.reshape(slot_count * tokens, 4 * enc_width).astype(F32)
    proj_scale = norm_scale(merged)
    proj_normed = (merged * proj_scale).astype(BF)
    proj_pre = dot_nn(proj_normed, proj_in)
    scale_row = jnp.concatenate(
        [part[:, 0] for part in split_pair(enc_scale) + split_pair(proj_scale)]
    )
    scale_row = jnp.pad(scale_row, (0, 16 * rank - scale_row.shape[0])).reshape(16, rank)
    payload = jnp.concatenate(
        [
            text_down, text_up, cot_up, enc_pre.astype(BF), enc_inner.astype(BF),
            proj_pre.astype(BF), scale_row,
        ],
        axis=0,
    )
    gath = section_gather(payload)

    image_rows = lax.dynamic_slice_in_dim(proj_out, grp * piece, piece, 0)
    rows = jnp.concatenate([image_rows[None], up_rows], axis=0).reshape(-1, width)
    gram = jnp.stack(
        [
            dot_nn(rows, weight_down).reshape(sections + 1, piece, rank),
            dot_nt(rows, weight_up).reshape(sections + 1, piece, rank),
        ],
        axis=1,
    ).astype(BF).reshape(-1, rank)
    every_gram = lax.all_gather(gram, ("section", "dp"), axis=0)

    patch_cols = lax.all_to_all(patches, "section", 1, 0, tiled=True)
    normed_cols = lax.all_to_all(proj_normed, "section", 1, 0, tiled=True)
    text_late, cot_late, _ = lax.optimization_barrier((text, cot, gram))
    text_cols = lax.all_to_all(text_late, "dp", 1, 0, tiled=True)
    cot_cols = lax.all_to_all(cot_late, "dp", 1, 0, tiled=True)
    share = width // groups
    own_slices = jnp.concatenate(
        [
            lax.dynamic_slice_in_dim(weight_down, grp * share, share, 0).T,
            lax.dynamic_slice_in_dim(weight_up, grp * share, share, 1),
        ],
        axis=0,
    )
    own_slices, every_gram = lax.optimization_barrier((own_slices, every_gram))
    slices = lax.all_gather(own_slices, "section", axis=0)
    down_slices = slices[:, :rank].reshape(-1, share)
    up_slices = jnp.concatenate(
        [
            lax.dynamic_slice_in_dim(proj_out, grp * share, share, 1),
            slices[:, rank:].reshape(-1, share),
        ],
        axis=0,
    )

    coef, factor, image = rank_space(
        sec, every_gram, gath, cot_image, text_norm, image_gram, sel, width
    )
    d_proj, placed, placed_scaled = image[0], image[1], image[2]
    factors = lax.all_gather(factor, "dp", axis=0)
    coef = lax.all_to_all(coef.reshape(groups, -1, rank), "dp", 0, 0)
    coef = jnp.sum(coef.astype(F32), axis=0).astype(BF)
    coef = lax.all_gather(coef, "dp", axis=0, tiled=True)

    at = 3 * rank
    many = slot_count * patch_count
    group_enc_pre = gath[:, at:at + many].reshape(-1, rank).astype(F32)
    group_inner = gath[:, at + many:at + 2 * many].reshape(-1, rank).astype(F32)
    at += 2 * many
    few = slot_count * tokens
    group_proj_pre = gath[:, at:at + few].reshape(-1, rank).astype(F32)
    scales = gath[:, at + few:].reshape(sections, -1).astype(F32)
    group_enc_scale = (scales[:, :many] + scales[:, many:2 * many]).reshape(-1, 1)
    group_proj_scale = (
        scales[:, 2 * many:2 * many + few] + scales[:, 2 * many + few:2 * many + 2 * few]
    ).reshape(-1, 1)
    group_act = gelu_tanh(group_enc_pre).astype(BF)
    block = enc_width // sections
    own_up = lax.dynamic_slice_in_dim(enc_up, sec * block, block, 1)
    out_cols = (patch_cols.astype(F32) + dot_nn(group_act, own_up)).astype(BF)
    enc_cols = (patch_cols.astype(F32) * group_enc_scale).astype(BF)
    quarters = proj_in.reshape(4, enc_width, rank)
    cross = jnp.einsum("ker,qe->rkq", quarters, enc_up, preferred_element_type=F32).astype(BF)
    own_in = lax.dynamic_slice_in_dim(quarters, sec * block, block, 1)
    cot_block = lax.dynamic_slice_in_dim(cot, sec * (width // sections), width // sections, 1)
    out_block = lax.dynamic_slice_in_dim(proj_out, sec * (width // sections), width // sections, 1)

    d_proj32 = d_proj.astype(F32)
    mean = jnp.sum(d_proj32 * group_proj_pre, axis=1, keepdims=True) / (4 * enc_width)
    d_scaled = (d_proj32 * group_proj_scale).astype(BF)
    pull = jnp.repeat(mean * group_proj_scale * group_proj_scale, 4, axis=0)
    d_enc = dot_nn(d_scaled, cross.reshape(rank, -1)).reshape(-1, rank)
    d_enc = ((d_enc - pull * group_inner) * gelu_slope(group_enc_pre)).astype(BF)
    part_enc_down = dot_tn(enc_cols, d_enc)
    inner = jnp.einsum(
        "ir,ika->kra", d_scaled, group_act.reshape(-1, 4, rank), preferred_element_type=F32
    ).astype(BF)
    part_enc_up = jnp.einsum("ker,kra->ea", own_in, inner, preferred_element_type=F32)
    part_enc_up = part_enc_up - dot_tn(out_cols, (pull * group_act.astype(F32)).astype(BF))
    part_proj_in = dot_tn(normed_cols, d_proj)
    part_out = dot_tn(cot_block, placed) - dot_tn(
        out_block, dot_tn(placed, placed_scaled).astype(BF)
    )
    parts = jnp.concatenate(
        [
            part.astype(BF).reshape(groups, -1, rank)
            for part in (part_enc_down, part_enc_up, part_proj_in, part_out)
        ],
        axis=1,
    )
    parts = jnp.sum(lax.all_to_all(parts, "dp", 0, 0).astype(F32), axis=0)
    n_enc = block // groups
    n_in = 4 * n_enc
    grad_enc_down = parts[:n_enc]
    grad_enc_up = parts[n_enc:2 * n_enc].T
    grad_proj_in = parts[2 * n_enc:2 * n_enc + n_in]
    own_out = parts[2 * n_enc + n_in:]

    tall = (sections + 1) * rank
    layer_of = jnp.arange(tall, dtype=jnp.int32)[:, None] // rank - 1
    pair_coef = coef[:tall]
    self_coef = coef[tall:]
    zero = jnp.zeros_like(pair_coef)
    low_coef = jnp.where(layer_of < sec, pair_coef, zero)
    high_coef = jnp.where(layer_of > sec, pair_coef, zero)[rank:]
    all_grad = factors[:, 0].reshape(-1, rank)
    all_act = factors[:, 1].reshape(-1, rank)
    all_scaled = factors[:, 2].reshape(-1, rank)
    grad_dec_down = dot_tn(text_cols, all_grad) + dot_tn(up_slices, low_coef)
    grad_dec_up = (
        dot_tn(all_act, cot_cols)
        - dot_tn(all_scaled, text_cols)
        + dot_tn(high_coef, down_slices)
        - dot_tn(self_coef, up_slices)
    )

    few_cols = width // (sections * groups)
    down_pick = lax.dynamic_slice_in_dim(
        weight_down.reshape(sections, -1, rank), grp * few_cols, few_cols, 1
    ).reshape(-1, rank)
    up_pick = lax.dynamic_slice_in_dim(
        weight_up.reshape(rank, sections, -1), grp * few_cols, few_cols, 2
    ).reshape(rank, -1)
    term = dot_nt(down_pick, pair_coef[:rank]) - dot(up_pick, self_coef[:rank], (0, 1))
    term = lax.all_to_all(term.astype(BF).reshape(sections, few_cols, rank), "section", 0, 0)
    grad_proj_out = (own_out + jnp.sum(term.astype(F32), axis=0)).T
    return (
        grad_dec_down[None],
        grad_dec_up[None],
        grad_enc_down,
        grad_enc_up,
        grad_proj_in,
        grad_proj_out,
    )


def solution(mesh):
    placed = (
        P("dp", None, None),
        P("dp", None, None),
        P("section", None, None),
        P("section", None, None),
        P("dp", "section", None, None, None),
        P(),
        P(),
        P(),
        P(),
        P("dp", None),
    )
    return jax.shard_map(
        shards,
        mesh=mesh,
        in_specs=placed,
        out_specs=(
            P("section", "dp", None),
            P("section", None, "dp"),
            P(("section", "dp"), None),
            P(None, ("section", "dp")),
            P(("section", "dp"), None),
            P(None, ("section", "dp")),
        ),
        check_vma=False,
    )
```

```python
import functools

import jax
import jax.numpy as jnp
from jax import lax
from jax.experimental import pallas as pl
from jax.experimental.pallas import tpu as pltpu
from jax.sharding import PartitionSpec as P

EPS = 1e-06
GELU_C = 0.7978845608028654
BF = jnp.bfloat16
F32 = jnp.float32


def gelu_tanh(value):
    return 0.5 * value * (1.0 + jnp.tanh(GELU_C * (value + 0.044715 * value * value * value)))


def gelu_slope(value):
    inner = jnp.tanh(GELU_C * (value + 0.044715 * value * value * value))
    return 0.5 * (1.0 + inner) + 0.5 * value * (1.0 - inner * inner) * GELU_C * (
        1.0 + 3.0 * 0.044715 * value * value
    )


def norm_scale(rows32):
    return lax.rsqrt(jnp.mean(rows32 * rows32, axis=-1, keepdims=True) + EPS)


def dot(left, right, dims):
    return lax.dot_general(left, right, ((dims[:1], dims[1:]), ((), ())), preferred_element_type=F32)


def dot_nn(left, right):
    return dot(left, right, (1, 0))


def dot_tn(left, right):
    return dot(left, right, (0, 0))


def dot_nt(left, right):
    return dot(left, right, (1, 1))


RANK = 128
VMEM = pl.BlockSpec(memory_space=pltpu.VMEM)
SMEM = pl.BlockSpec(memory_space=pltpu.SMEM)
PARAMS = pltpu.CompilerParams(vmem_limit_bytes=48 * 1024 * 1024)


def scalars(*values):
    return jnp.stack(values).astype(jnp.int32)


def text_kernel(
    steps, kept,
    start_ref, keep_ref, text_ref, cot_ref, down_ref, up_ref, out_ref,
    cols_ref, proj_ref, image_ref, norm_ref, gram_ref,
    proj, image, gram,
):
    step = pl.program_id(0)

    @pl.when(step == 0)
    def _():
        proj[...] = jnp.zeros_like(proj)
        image[...] = jnp.zeros_like(image)
        gram[...] = jnp.zeros_like(gram)
        norm_ref[...] = jnp.zeros_like(norm_ref)

    rows = text_ref.shape[0]
    text32 = text_ref[...].astype(F32) * keep_ref[...]
    text = text32.astype(BF)
    cot = cot_ref[...]
    norm_ref[...] += jnp.sum(text32 * text32, axis=1, keepdims=True)
    proj[:RANK] += dot_nn(text, down_ref[...])
    proj[RANK:2 * RANK] += dot_nt(text, up_ref[...])
    proj[2 * RANK:] += dot_nt(cot, up_ref[...])
    image[...] += dot_nt(cot, out_ref[...])
    gram[...] += dot_nt(out_ref[...], out_ref[...])

    @pl.when(step < kept)
    def _():
        cols_ref[0, :rows, :] = text
        cols_ref[0, rows:, :] = cot

    @pl.when(step == steps - 1)
    def _():
        proj_ref[...] = proj[...].astype(BF)
        image_ref[...] = image[...]
        gram_ref[...] = gram[...].astype(BF)


def text_products(start, keep, text, cot, down, up, out, groups):
    rows, width = text.shape
    share = width // groups
    kept = groups // 2
    across = pl.BlockSpec((rows, share), lambda i, at: (0, (at[0] + i) % groups))
    fixed = pl.BlockSpec((rows, RANK), lambda i, at: (0, 0))
    column = pl.BlockSpec((rows, 1), lambda i, at: (0, 0))
    return pl.pallas_call(
        functools.partial(text_kernel, groups, kept),
        grid_spec=pltpu.PrefetchScalarGridSpec(
            num_scalar_prefetch=1,
            grid=(groups,),
            in_specs=[
                column,
                across,
                across,
                pl.BlockSpec((share, RANK), lambda i, at: ((at[0] + i) % groups, 0)),
                across,
                across,
            ],
            out_specs=[
                pl.BlockSpec(
                    (1, 2 * rows, share), lambda i, at: (jnp.minimum(i, kept - 1), 0, 0)
                ),
                pl.BlockSpec((3 * RANK, RANK), lambda i, at: (0, 0)),
                fixed,
                column,
                fixed,
            ],
            scratch_shapes=[
                pltpu.VMEM((3 * RANK, RANK), F32),
                pltpu.VMEM((rows, RANK), F32),
                pltpu.VMEM((RANK, RANK), F32),
            ],
        ),
        out_shape=[
            jax.ShapeDtypeStruct((kept, 2 * rows, share), BF),
            jax.ShapeDtypeStruct((3 * RANK, RANK), BF),
            jax.ShapeDtypeStruct((rows, RANK), F32),
            jax.ShapeDtypeStruct((rows, 1), F32),
            jax.ShapeDtypeStruct((RANK, RANK), BF),
        ],
        compiler_params=PARAMS,
    )(scalars(start), keep, text, cot, down, up, out)


def two_lanes(column):
    high = column.astype(BF).astype(F32)
    lane = lax.broadcasted_iota(jnp.int32, (column.shape[0], RANK), 1)
    zero = jnp.zeros((column.shape[0], RANK), F32)
    return jnp.where(lane == 0, high, jnp.where(lane == 1, column - high, zero)).astype(BF)


def front_kernel(
    sections, windows, in_windows,
    place_ref, patch_ref, down_ref, up_ref, in_ref,
    pre_ref, cols_ref, cross_ref,
    patch, enc, inner, state, tiles,
):
    rows, width = patch_ref.shape
    count = width // RANK
    quarter = rows // 4

    def keep_tiles(ref, value):
        for m in range(count):
            ref[m] = value[:, m * RANK:(m + 1) * RANK]

    def fourth(ref, k):
        return jnp.concatenate(
            [ref[m, pl.ds(k, quarter, stride=4), :] for m in range(count)], axis=1
        )

    patch32 = patch_ref[...].astype(F32)
    keep_tiles(patch, patch32)
    scale = norm_scale(patch32)
    pre = dot_nn((patch32 * scale).astype(BF), down_ref[...])
    act = gelu_tanh(pre).astype(BF)
    out = (patch32 + dot_nn(act, up_ref[...])).astype(BF)
    keep_tiles(enc, out.astype(F32))
    inner[...] = dot_nt(out, up_ref[...])
    state[...] = pre
    total = jnp.zeros((quarter, 1), F32)
    for k in range(4):
        part = fourth(enc, k)
        total = total + jnp.sum(part * part, axis=1, keepdims=True)
    merged_scale = lax.rsqrt(total * (1.0 / (4 * width)) + EPS)
    proj = jnp.zeros((quarter, RANK), F32)
    for k in range(4):
        normed = (fourth(enc, k) * merged_scale).astype(BF)
        proj = proj + dot_nn(normed, in_ref[k])
        cross_ref[:, k * RANK:(k + 1) * RANK] = dot(in_ref[k], up_ref[...], (0, 1)).astype(BF)
        for m in range(count):
            tiles[k, m] = normed[:, m * RANK:(m + 1) * RANK]
        head = [
            state[pl.ds(k, quarter, stride=4), :].astype(BF),
            inner[pl.ds(k, quarter, stride=4), :].astype(BF),
            two_lanes(norm_scale(fourth(patch, k))),
        ]
        for step in range(sections):
            for at, value in enumerate(head):
                cols_ref[step, at * rows + k * quarter:at * rows + (k + 1) * quarter, :] = value
    merged_lanes = two_lanes(merged_scale)
    for step in range(sections):
        to = lax.rem(place_ref[0] + step, sections)
        base = 3 * rows
        cols_ref[step, base:base + quarter, :] = merged_lanes
        base += quarter
        for m in range(windows[1]):
            for k in range(4):
                tile = patch[to * (windows[0] // RANK) + m, pl.ds(k, quarter, stride=4), :]
                at = base + m * rows + k * quarter
                cols_ref[step, at:at + quarter, :] = tile.astype(BF)
        base += windows[1] * rows
        per = sections // 4
        for m in range(in_windows[1]):
            tile = tiles[to // per, lax.rem(to, per) * (in_windows[0] // RANK) + m]
            cols_ref[step, base + m * quarter:base + (m + 1) * quarter, :] = tile
    pre_ref[...] = proj.astype(BF)


def window(width, count):
    block = width // count
    stride = block // RANK * RANK
    tiles = -(-((count - 1) * (block - stride) + block) // RANK)
    return stride, tiles


def encoder_front(sec, patches, enc_down, enc_up, proj_in, sections):
    rows, width = patches.shape
    windows = window(width, sections)
    in_windows = window(width, sections // 4)
    total = 3 * rows + rows // 4 + windows[1] * rows + in_windows[1] * (rows // 4)
    return pl.pallas_call(
        functools.partial(front_kernel, sections, windows, in_windows),
        in_specs=[SMEM] + [VMEM] * 4,
        out_specs=[VMEM] * 3,
        out_shape=[
            jax.ShapeDtypeStruct((rows // 4, RANK), BF),
            jax.ShapeDtypeStruct((sections, total, RANK), BF),
            jax.ShapeDtypeStruct((RANK, 4 * RANK), BF),
        ],
        scratch_shapes=[
            pltpu.VMEM((width // RANK, rows, RANK), F32),
            pltpu.VMEM((width // RANK, rows, RANK), F32),
            pltpu.VMEM((rows, RANK), F32),
            pltpu.VMEM((rows, RANK), F32),
            pltpu.VMEM((4, width // RANK, rows // 4, RANK), BF),
        ],
        compiler_params=PARAMS,
    )(scalars(sec), patches, enc_down, enc_up, proj_in)


def pack_kernel(layers, core_ref, gram_ref, out_ref, packed):
    at = 0
    for l in range(layers):
        size = (l + 2) * 16
        packed[at:at + size, :] = gram_ref[l, :size, :]
        at += size
    half = at // 2
    value = packed[pl.ds(pl.multiple_of(core_ref[0] * half, 16), half), :]
    for to in range(out_ref.shape[0]):
        out_ref[to] = value


def pack_gram(core, gram, groups):
    layers = gram.shape[0]
    total = sum((l + 2) * 16 for l in range(layers))
    return pl.pallas_call(
        functools.partial(pack_kernel, layers),
        in_specs=[SMEM, VMEM],
        out_specs=VMEM,
        out_shape=jax.ShapeDtypeStruct((groups, total // 2, RANK), BF),
        scratch_shapes=[pltpu.VMEM((total, RANK), BF)],
        compiler_params=PARAMS,
    )(scalars(core), gram)


def rank_kernel(
    layers, width,
    place_ref, own_ref, other_ref, gath_ref, cot_ref, norm_ref, image_gram_ref, sel_ref,
    coef_ref, factor_ref, image_ref,
    weight, acts, act_cat, grads, scaled, back, pre_ref, slope_ref, inner_ref, scale_ref,
):
    rank = RANK
    own = place_ref[0]
    core = place_ref[1]
    at = 0
    for l in range(layers):
        for j in range(l + 2):
            which, place = divmod(at, own_ref.shape[1])
            span = slice(place, place + 16)
            tile = jnp.where(core == which, own_ref[:, span, :], other_ref[:, span, :])
            tile = tile.astype(F32)
            rows = slice(j * rank, (j + 1) * rank)
            weight[l, rows, :rank] = tile[:, :8, :].reshape(rank, rank).astype(BF)
            weight[l, rows, rank:] = tile[:, 8:, :].reshape(rank, rank).astype(BF)
            at += 16

    proj_half = jnp.concatenate(
        [gath_ref[l, 3 * rank:3 * rank + 16, :] for l in range(layers)], axis=0
    )
    proj_pre = proj_half.astype(F32)
    sel = sel_ref[...]
    placed = dot_nn(sel, gelu_tanh(proj_pre).astype(BF))
    placed_half = placed.astype(BF)
    acts[0] = placed_half
    act_cat[:, :rank] = placed_half
    image_inner = dot_nn(placed_half, image_gram_ref[...])
    total = norm_ref[...] + jnp.sum(placed * image_inner, axis=1, keepdims=True)
    for l in range(layers):
        here = (l + 1) * rank
        scale = lax.rsqrt(jnp.maximum(total, 0.0) * (1.0 / width) + EPS)
        both = dot_nn(act_cat[:, :here], weight[l, :here, :])
        pre = scale * (gath_ref[l, :rank, :].astype(F32) + both[:, :rank])
        inner = gath_ref[l, rank:2 * rank, :].astype(F32) + both[:, rank:]
        sig = jax.nn.sigmoid(pre)
        act = (pre * sig).astype(BF)
        acts[l + 1] = act
        act_cat[:, here:here + rank] = act
        after = inner + dot_nn(act, weight[l, here:here + rank, rank:])
        total = total + jnp.sum(act.astype(F32) * (inner + after), axis=1, keepdims=True)
        pre_ref[l] = pre
        slope_ref[l] = sig * (1.0 + pre * (1.0 - sig))
        inner_ref[l] = after
        scale_ref[l] = scale
    back[...] = jnp.zeros_like(back)
    sums = jnp.zeros_like(total)
    for l in reversed(range(layers)):
        here = (l + 1) * rank
        cot = gath_ref[l, 2 * rank:3 * rank, :].astype(F32)
        d_act = cot - sums * inner_ref[l] + back[:, here:here + rank]
        d_pre = (d_act * slope_ref[l]).astype(BF).astype(F32)
        scale = scale_ref[l]
        mean = jnp.sum(d_pre * pre_ref[l], axis=1, keepdims=True) * (1.0 / width)
        grad = (scale * d_pre).astype(BF)
        part = (sums * acts[l + 1].astype(F32)).astype(BF)
        grads[l] = grad
        scaled[l + 1] = part
        pair = jnp.concatenate([grad, -part], axis=1)
        back[:, :here] += dot_nt(pair, weight[l, :here, :])
        sums = sums + scale * scale * mean
    d_image = cot_ref[...] - sums * image_inner + back[:, :rank]
    scaled[0] = (sums * placed).astype(BF)
    d_slot = dot_tn(sel, d_image.astype(BF))
    image_ref[0] = (d_slot * gelu_slope(proj_pre)).astype(BF)
    image_ref[1] = placed_half
    image_ref[2] = scaled[0]
    image_ref[3] = proj_half

    own_act = acts[own + 1]
    own_grad = grads[own]
    own_scaled = scaled[own + 1]
    factor_ref[0] = own_grad
    factor_ref[1] = own_act
    factor_ref[2] = own_scaled
    coef_ref[0] = dot_tn(acts[0], own_grad).astype(BF)
    for l in range(layers):
        low = l < own
        left = jnp.where(low, acts[l + 1], grads[l])
        right = jnp.where(low, own_grad, own_act)
        coef_ref[l + 1] = dot_tn(left, right).astype(BF)
    for l in range(layers + 1):
        low = l <= own + 1
        left = jnp.where(low, acts[l], scaled[l])
        right = jnp.where(low, own_scaled, own_act)
        coef_ref[layers + 1 + l] = dot_tn(left, right).astype(BF)


def rank_space(position, core, gram, other, gath, cot, norms, image_gram, sel, width):
    layers = gath.shape[0]
    rank = RANK
    tall = (layers + 1) * rank
    return pl.pallas_call(
        functools.partial(rank_kernel, layers, width),
        in_specs=[SMEM] + [VMEM] * 7,
        out_specs=[VMEM] * 3,
        out_shape=[
            jax.ShapeDtypeStruct((2 * layers + 2, rank, rank), BF),
            jax.ShapeDtypeStruct((3, rank, rank), BF),
            jax.ShapeDtypeStruct((4, rank, rank), BF),
        ],
        scratch_shapes=[
            pltpu.VMEM((layers, tall, 2 * rank), BF),
            pltpu.VMEM((layers + 1, rank, rank), BF),
            pltpu.VMEM((rank, tall), BF),
            pltpu.VMEM((layers, rank, rank), BF),
            pltpu.VMEM((layers + 1, rank, rank), BF),
            pltpu.VMEM((rank, tall), F32),
            pltpu.VMEM((layers, rank, rank), F32),
            pltpu.VMEM((layers, rank, rank), F32),
            pltpu.VMEM((layers, rank, rank), F32),
            pltpu.VMEM((layers, rank, 1), F32),
        ],
        compiler_params=PARAMS,
    )(scalars(position, core), gram, other, gath, cot, norms, image_gram, sel)


def late_kernel(sections, enc_width, tiles, in_tiles, pieces, shift_ref, *refs):
    cols_refs = refs[:sections]
    image_ref, cross_ref, up_ref, in_ref, cot_ref, out_ref, part_ref = refs[sections:sections + 7]
    down, up, proj, last = refs[sections + 7:]
    few = RANK // sections
    many = 4 * few

    def arrived(index):
        rows = []
        for step in range(sections):
            source = lax.rem(shift_ref[3] + sections - step, sections)
            rows.append(image_ref[index, pl.ds(pl.multiple_of(source * few, few), few), :])
        return jnp.concatenate(rows, axis=0)

    d_proj = arrived(0)
    placed = image_ref[1]
    d_proj32 = d_proj.astype(F32)
    proj_pre = arrived(3).astype(F32)

    def group(start):
        return jnp.concatenate(
            [ref[start:start + few, :] for ref in cols_refs], axis=0
        )

    proj_scale = jnp.sum(group(3 * many).astype(F32), axis=1, keepdims=True)
    mean = jnp.sum(d_proj32 * proj_pre, axis=1, keepdims=True) * (1.0 / (4 * enc_width))
    d_scaled = (d_proj32 * proj_scale).astype(BF)
    pull = mean * proj_scale * proj_scale
    for k in range(4):
        at = k * few
        enc_pre = group(at).astype(F32)
        inner = group(many + at).astype(F32)
        scale = jnp.sum(group(2 * many + at).astype(F32), axis=1, keepdims=True)
        act = gelu_tanh(enc_pre).astype(BF)
        d_enc = dot_nn(d_scaled, cross_ref[:, k * RANK:(k + 1) * RANK]) - pull * inner
        d_enc = (d_enc * gelu_slope(enc_pre)).astype(BF)
        pulled = (pull * act.astype(F32)).astype(BF)
        value = dot_nn(in_ref[k], dot_tn(d_scaled, act).astype(BF))
        if k == 0:
            up[:tiles * RANK, :] = value
        else:
            up[:tiles * RANK, :] += value
        for m in range(tiles):
            rows = slice(m * RANK, (m + 1) * RANK)
            patch = group(3 * many + few + m * many + at).astype(F32)
            out = (patch + dot_nn(act, up_ref[:, rows])).astype(BF)
            up[rows, :] -= dot_tn(out, pulled)
            value = dot_tn((patch * scale).astype(BF), d_enc)
            if k == 0:
                down[rows, :] = value
            else:
                down[rows, :] += value
    base = 3 * many + few + tiles * many
    for m in range(in_tiles):
        proj[m * RANK:(m + 1) * RANK, :] = dot_tn(group(base + m * few), d_proj)
    last[...] = dot_tn(cot_ref[...], placed) - dot_tn(
        out_ref[...], dot_tn(placed, image_ref[2]).astype(BF)
    )
    groups = part_ref.shape[0]
    n_enc, n_in, pad_enc, pad_in = pieces
    n_out = last.shape[0] // groups
    for step in range(groups):
        to = lax.rem(shift_ref[2] + step, groups)
        at = shift_ref[0] + n_enc * to
        part_ref[step, :pad_enc, :] = down[pl.ds(at, pad_enc), :].astype(BF)
        part_ref[step, pad_enc:2 * pad_enc, :] = up[pl.ds(at, pad_enc), :].astype(BF)
        at = shift_ref[1] + n_in * to
        part_ref[step, 2 * pad_enc:2 * pad_enc + pad_in, :] = proj[pl.ds(at, pad_in), :].astype(BF)
        at = pl.multiple_of(to * n_out, n_out)
        part_ref[step, 2 * pad_enc + pad_in:, :] = last[pl.ds(at, n_out), :].astype(BF)


def encoder_late(sec, grp, cols, image, cross, own_up, own_in, cot, out, enc_width, groups):
    sections = len(cols)
    tiles = window(enc_width, sections)[1]
    in_tiles = window(enc_width, sections // 4)[1]
    n_enc = enc_width // sections // groups
    n_in = 4 * n_enc
    pad_enc = -(-n_enc // 16) * 16
    pad_in = -(-n_in // 16) * 16
    block = enc_width // sections
    in_block = 4 * block
    shifts = scalars(
        sec * (block % RANK), (sec % (sections // 4)) * (in_block % RANK), grp, sec
    )
    n_out = out.shape[1] // groups
    total = 2 * pad_enc + pad_in + n_out
    parts = pl.pallas_call(
        functools.partial(
            late_kernel, sections, enc_width, tiles, in_tiles, (n_enc, n_in, pad_enc, pad_in)
        ),
        in_specs=[SMEM] + [VMEM] * (sections + 6),
        out_specs=VMEM,
        out_shape=jax.ShapeDtypeStruct((groups, total, RANK), BF),
        scratch_shapes=[
            pltpu.VMEM((tiles * RANK + 16, RANK), F32),
            pltpu.VMEM((tiles * RANK + 16, RANK), F32),
            pltpu.VMEM((in_tiles * RANK + 16, RANK), F32),
            pltpu.VMEM((out.shape[1], RANK), F32),
        ],
        compiler_params=PARAMS,
    )(shifts, *cols, image, cross, own_up, own_in, cot, out)
    return parts, (n_enc, n_in, pad_enc, pad_in)


def sum_kernel(count, *refs):
    total = refs[0][...].astype(F32)
    for ref in refs[1:count]:
        total = total + ref[...].astype(F32)
    refs[count][...] = total


def sum_parts(parts):
    return pl.pallas_call(
        functools.partial(sum_kernel, len(parts)),
        in_specs=[VMEM] * len(parts),
        out_specs=VMEM,
        out_shape=jax.ShapeDtypeStruct(parts[0].shape, F32),
        compiler_params=PARAMS,
    )(*parts)


def last_kernel(layers, groups, place_ref, *refs):
    blocks = refs[:groups]
    factor_ref, coef_ref, down_ref, up_ref, out_ref, grad_down_ref, grad_up_ref = refs[groups:]
    sec, grp, core = place_ref[0], place_ref[1], place_ref[2]
    rows = blocks[0].shape[0] // 2
    half = groups // 2
    share = blocks[0].shape[1]
    total_down = jnp.zeros((share, RANK), F32)
    total_up = jnp.zeros((RANK, share), F32)
    for at, block in enumerate(blocks):
        part = core if at < half else 1 - core
        source = lax.rem(grp + 2 * groups - half * part - at % half, groups)
        text = block[:rows, :]
        total_down += dot_tn(text, factor_ref[source, 0])
        total_up += dot_tn(factor_ref[source, 1], block[rows:, :])
        total_up -= dot_tn(factor_ref[source, 2], text)
    total_down += dot_tn(out_ref[...], coef_ref[0])
    total_up -= dot_tn(coef_ref[layers + 1], out_ref[...])
    turned = jnp.zeros((share, RANK), F32)
    for l in range(layers):
        coef = coef_ref[l + 1]
        zero = jnp.zeros_like(coef)
        total_down += dot_tn(up_ref[l], jnp.where(l < sec, coef, zero))
        turned += dot_nn(down_ref[l], jnp.where(l > sec, coef, zero))
        total_up -= dot_tn(coef_ref[layers + 2 + l], up_ref[l])
    grad_down_ref[...] = total_down
    grad_up_ref[...] = total_up + turned.T


def last_products(sec, grp, core, blocks, factors, coef, down, up, out):
    layers = down.shape[0]
    share = out.shape[1]
    groups = len(blocks)
    return pl.pallas_call(
        functools.partial(last_kernel, layers, groups),
        in_specs=[SMEM] + [VMEM] * (groups + 5),
        out_specs=[VMEM] * 2,
        out_shape=[
            jax.ShapeDtypeStruct((share, RANK), F32),
            jax.ShapeDtypeStruct((RANK, share), F32),
        ],
        compiler_params=PARAMS,
    )(scalars(sec, grp, core), *blocks, factors, coef, down, up, out)


def spread(value, axis):
    count = lax.axis_size(axis)
    return lax.all_to_all(jnp.broadcast_to(value[None], (count,) + value.shape), axis, 0, 0)


def shards(text, cotangent, dec_down, dec_up, images, enc_down, enc_up, proj_in, proj_out, frame):
    sections = lax.axis_size("section")
    groups = lax.axis_size("dp")
    sec = lax.axis_index("section")
    grp = lax.axis_index("dp")
    core = sec % 2
    both = ("section", "dp")
    slot_count, patch_count, enc_width = images.shape[2:]
    tokens = patch_count // 4
    rows_total, width = text.shape[1:]
    rank = dec_down.shape[2]
    weight_down = dec_down[0]
    weight_up = dec_up[0]
    frames = frame[0]
    text = text[0]
    cot = cotangent[0]
    piece = rank // groups
    share = width // groups
    half = groups // 2
    swap = [(at, at ^ 1) for at in range(sections)]

    up_rows = spread(lax.dynamic_slice_in_dim(weight_up, grp * piece, piece, 0), "section")

    slot_row = jnp.repeat(frames, tokens)[None, :]
    row = jnp.arange(rows_total, dtype=jnp.int32)[:, None]
    column = jnp.arange(rows_total, dtype=jnp.int32)[None, :]
    sel = (slot_row == row // tokens) & (row % tokens == column % tokens)
    keep = 1.0 - jnp.any(sel, axis=1, keepdims=True).astype(F32)
    sel = sel.astype(BF)
    cols, proj, cot_image, text_norm, image_gram = text_products(
        grp + half * core, keep, text, cot, weight_down, weight_up, proj_out, groups
    )

    patches = images[0, 0].reshape(slot_count * patch_count, enc_width)
    quarters = proj_in.reshape(4, enc_width, rank)
    proj_pre, enc_cols, cross = encoder_front(
        sec, patches, enc_down, enc_up, quarters, sections
    )
    gath = lax.all_gather(jnp.concatenate([proj, proj_pre], axis=0), "section", axis=0)

    image_rows = lax.dynamic_slice_in_dim(proj_out, grp * piece, piece, 0)
    up_rows, cols, enc_cols = lax.optimization_barrier((up_rows, cols, enc_cols))
    rows = jnp.concatenate([image_rows[None], up_rows], axis=0).reshape(-1, width)
    gram = jnp.stack(
        [
            dot_nn(rows, weight_down).reshape(sections + 1, piece, rank),
            dot_nt(rows, weight_up).reshape(sections + 1, piece, rank),
        ],
        axis=1,
    ).astype(BF).reshape(-1, rank)
    gram, cols = lax.optimization_barrier((gram, cols))
    packed = pack_gram(core, spread(gram, "section"), groups)

    blocks = []
    for step in range(half):
        pairs = []
        for at in range(sections):
            for source in range(groups):
                to = (source + half * (at % 2) + step) % groups
                pairs.append((at * groups + source, at * groups + to))
        blocks.append(lax.ppermute(cols[step], both, pairs))

    packed, enc_cols = lax.optimization_barrier((packed, enc_cols))
    own_gram = lax.all_to_all(packed, "dp", 0, 0)
    other_gram = lax.ppermute(own_gram, "section", swap)

    window_parts = [enc_cols[0]]
    for step in range(1, sections):
        pairs = [(at, (at + step) % sections) for at in range(sections)]
        window_parts.append(lax.ppermute(enc_cols[step], "section", pairs))

    blocks = blocks + [lax.ppermute(block, "section", swap) for block in blocks]

    own_down = lax.dynamic_slice_in_dim(weight_down, grp * share, share, 0)
    own_up = lax.dynamic_slice_in_dim(weight_up, grp * share, share, 1)
    own_down, own_up, gath = lax.optimization_barrier((own_down, own_up, gath))
    down_slices = lax.all_gather(own_down, "section", axis=0)
    up_slices = lax.all_gather(own_up, "section", axis=0)
    out_slice = lax.dynamic_slice_in_dim(proj_out, grp * share, share, 1)
    stride, tiles = window(enc_width, sections)
    wide = width // sections
    few_cols = width // (sections * groups)
    early = (
        out_slice,
        lax.dynamic_slice_in_dim(enc_up, sec * stride, tiles * rank, 1),
        lax.dynamic_slice_in_dim(quarters, sec * stride, tiles * rank, 1),
        lax.dynamic_slice_in_dim(cot, sec * wide, wide, 1),
        lax.dynamic_slice_in_dim(proj_out, sec * wide, wide, 1),
        lax.dynamic_slice_in_dim(
            weight_down.reshape(sections, -1, rank), grp * few_cols, few_cols, 1
        ).reshape(-1, rank),
        lax.dynamic_slice_in_dim(
            weight_up.reshape(rank, sections, -1), grp * few_cols, few_cols, 2
        ).reshape(rank, -1),
    )
    early, gath = lax.optimization_barrier((early, gath))
    out_slice, up_window, in_window, cot_block, out_block, down_pick, up_pick = early

    coef, factor, image = rank_space(
        sec, core, own_gram, other_gram, gath, cot_image, text_norm, image_gram, sel, width
    )
    coef = lax.all_to_all(coef.reshape(groups, -1, rank), "dp", 0, 0)
    factors = lax.all_gather(factor, "dp", axis=0)

    parts, (n_enc, n_in, pad_enc, pad_in) = encoder_late(
        sec, grp, window_parts, image, cross, up_window, in_window, cot_block, out_block,
        enc_width, groups,
    )
    coef = jnp.sum(coef.astype(F32), axis=0).astype(BF)
    first = 6
    early_parts = [parts[step] for step in range(first)]
    late_parts, coef = lax.optimization_barrier((parts, coef))
    coef = spread(coef, "dp").reshape(-1, rank, rank)
    pieces = early_parts + [late_parts[step] for step in range(first, groups)]
    for step in range(1, groups):
        pairs = [(at, (at + step) % groups) for at in range(groups)]
        pieces[step] = lax.ppermute(pieces[step], "dp", pairs)
    parts = sum_parts(pieces)
    grad_enc_down = parts[:n_enc]
    grad_enc_up = parts[pad_enc:pad_enc + n_enc].T
    grad_proj_in = parts[2 * pad_enc:2 * pad_enc + n_in]
    own_out = parts[2 * pad_enc + pad_in:]

    term = dot_nt(down_pick, coef[0]) - dot(up_pick, coef[sections + 1], (0, 1))
    term = lax.all_to_all(term.astype(BF).reshape(sections, few_cols, rank), "section", 0, 0)

    grad_dec_down, grad_dec_up = last_products(
        sec, grp, core, blocks, factors, coef, down_slices, up_slices, out_slice
    )
    grad_proj_out = (own_out + jnp.sum(term.astype(F32), axis=0)).T
    return (
        grad_dec_down[None],
        grad_dec_up[None],
        grad_enc_down,
        grad_enc_up,
        grad_proj_in,
        grad_proj_out,
    )


def solution(mesh):
    placed = (
        P("dp", None, None),
        P("dp", None, None),
        P("section", None, None),
        P("section", None, None),
        P("dp", "section", None, None, None),
        P(),
        P(),
        P(),
        P(),
        P("dp", None),
    )
    return jax.shard_map(
        shards,
        mesh=mesh,
        in_specs=placed,
        out_specs=(
            P("section", "dp", None),
            P("section", None, "dp"),
            P(("section", "dp"), None),
            P(None, ("section", "dp")),
            P(("section", "dp"), None),
            P(None, ("section", "dp")),
        ),
        check_vma=False,
    )
```

```python
import functools

import jax
import jax.numpy as jnp
from jax import lax
from jax.experimental import pallas as pl
from jax.experimental.pallas import tpu as pltpu
from jax.sharding import PartitionSpec as P

EPS = 1e-06
GELU_C = 0.7978845608028654
BF = jnp.bfloat16
F32 = jnp.float32


def gelu_tanh(value):
    return 0.5 * value * (1.0 + jnp.tanh(GELU_C * (value + 0.044715 * value * value * value)))


def gelu_slope(value):
    inner = jnp.tanh(GELU_C * (value + 0.044715 * value * value * value))
    return 0.5 * (1.0 + inner) + 0.5 * value * (1.0 - inner * inner) * GELU_C * (
        1.0 + 3.0 * 0.044715 * value * value
    )


def norm_scale(rows32):
    return lax.rsqrt(jnp.mean(rows32 * rows32, axis=-1, keepdims=True) + EPS)


def dot(left, right, dims):
    return lax.dot_general(left, right, ((dims[:1], dims[1:]), ((), ())), preferred_element_type=F32)


def dot_nn(left, right):
    return dot(left, right, (1, 0))


def dot_tn(left, right):
    return dot(left, right, (0, 0))


def dot_nt(left, right):
    return dot(left, right, (1, 1))


RANK = 128
VMEM = pl.BlockSpec(memory_space=pltpu.VMEM)
SMEM = pl.BlockSpec(memory_space=pltpu.SMEM)
PARAMS = pltpu.CompilerParams(vmem_limit_bytes=48 * 1024 * 1024)


def scalars(*values):
    return jnp.stack(values).astype(jnp.int32)


def text_kernel(
    half, share, few, steps,
    place_ref, keep_ref, text_ref, cot_ref, down_ref, up_ref, out_ref,
    text_cols_ref, cot_cols_ref, proj_ref, image_ref, norm_ref, gram_ref,
    pick_ref, block_ref, slice_ref, out_slice_ref,
    proj, image, gram,
):
    step = pl.program_id(0)
    core, sec, grp = place_ref[0], place_ref[1], place_ref[2]

    @pl.when(step == 0)
    def _():
        proj[...] = jnp.zeros_like(proj)
        image[...] = jnp.zeros_like(image)
        gram[...] = jnp.zeros_like(gram)
        norm_ref[...] = jnp.zeros_like(norm_ref)

    text32 = text_ref[...].astype(F32) * keep_ref[...]
    text = text32.astype(BF)
    cot = cot_ref[...]
    norm_ref[...] += jnp.sum(text32 * text32, axis=1, keepdims=True)
    proj[:RANK] += dot_nn(text, down_ref[...])
    proj[RANK:2 * RANK] += dot_nt(text, up_ref[...])
    proj[2 * RANK:] += dot_nt(cot, up_ref[...])
    image[...] += dot_nt(cot, out_ref[...])
    gram[...] += dot_nt(out_ref[...], out_ref[...])

    own = pl.ds(pl.multiple_of(core * half, half), half)
    keep = keep_ref[own, :]
    pieces = text_cols_ref.shape[0]
    for piece in range(pieces):
        span = slice(piece * share, (piece + 1) * share)
        text_cols_ref[piece] = (text_ref[own, span].astype(F32) * keep).astype(BF)
        cot_cols_ref[piece] = cot_ref[own, span]

    pick_ref[0, 0] = down_ref[pl.ds(pl.multiple_of(grp * few, few), few), :]
    per = RANK // few
    lanes = up_ref[:, pl.ds(pl.multiple_of(grp // per * RANK, RANK), RANK)].astype(F32).T
    picked = lanes[:few]
    for at in range(1, per):
        picked = jnp.where(lax.rem(grp, per) == at, lanes[at * few:(at + 1) * few], picked)
    pick_ref[0, 1] = picked.astype(BF)

    @pl.when(step == sec)
    def _():
        block_ref[0] = cot
        block_ref[1] = out_ref[...]

    @pl.when(step == grp // pieces)
    def _():
        at = pl.multiple_of(lax.rem(grp, pieces) * share, share)
        slice_ref[:share, :] = down_ref[pl.ds(at, share), :]
        up = up_ref[:, pl.ds(at, share)]
        for m in range(share // RANK):
            slice_ref[share + m * RANK:share + (m + 1) * RANK, :] = up[:, m * RANK:(m + 1) * RANK]
        out_slice_ref[...] = out_ref[:, pl.ds(at, share)]

    @pl.when(step == steps - 1)
    def _():
        proj_ref[...] = proj[...].astype(BF)
        image_ref[...] = image[...]
        gram_ref[...] = gram[...].astype(BF)


def text_products(sec, grp, keep, text, cot, down, up, out, sections, groups):
    rows, width = text.shape
    share = width // groups
    steps = sections
    wide = width // steps
    pieces = wide // share
    few = wide // groups
    half = rows // 2
    across = pl.BlockSpec((rows, wide), lambda i: (0, i))
    fixed = pl.BlockSpec((rows, RANK), lambda i: (0, 0))
    column = pl.BlockSpec((rows, 1), lambda i: (0, 0))
    cols = pl.BlockSpec((pieces, half, share), lambda i: (i, 0, 0))
    return pl.pallas_call(
        functools.partial(text_kernel, half, share, few, steps),
        grid=(steps,),
        in_specs=[
            SMEM,
            column,
            across,
            across,
            pl.BlockSpec((wide, RANK), lambda i: (i, 0)),
            across,
            across,
        ],
        out_specs=[
            cols,
            cols,
            pl.BlockSpec((3 * RANK, RANK), lambda i: (0, 0)),
            fixed,
            column,
            fixed,
            pl.BlockSpec((1, 2, few, RANK), lambda i: (i, 0, 0, 0)),
            pl.BlockSpec((2, rows, wide), lambda i: (0, 0, 0)),
            pl.BlockSpec((2 * share, RANK), lambda i: (0, 0)),
            pl.BlockSpec((rows, share), lambda i: (0, 0)),
        ],
        out_shape=[
            jax.ShapeDtypeStruct((groups, half, share), BF),
            jax.ShapeDtypeStruct((groups, half, share), BF),
            jax.ShapeDtypeStruct((3 * RANK, RANK), BF),
            jax.ShapeDtypeStruct((rows, RANK), F32),
            jax.ShapeDtypeStruct((rows, 1), F32),
            jax.ShapeDtypeStruct((RANK, RANK), BF),
            jax.ShapeDtypeStruct((steps, 2, few, RANK), BF),
            jax.ShapeDtypeStruct((2, rows, wide), BF),
            jax.ShapeDtypeStruct((2 * share, RANK), BF),
            jax.ShapeDtypeStruct((rows, share), BF),
        ],
        scratch_shapes=[
            pltpu.VMEM((3 * RANK, RANK), F32),
            pltpu.VMEM((rows, RANK), F32),
            pltpu.VMEM((RANK, RANK), F32),
        ],
        compiler_params=PARAMS,
    )(scalars(sec % 2, sec, grp), keep, text, cot, down, up, out)


def window(width, count):
    block = width // count
    stride = block // RANK * RANK
    tiles = -(-((count - 1) * (block - stride) + block) // RANK)
    return stride, tiles


def front_kernel(
    sections, windows, in_windows,
    place_ref, image_ref, down_ref, up_ref, in_ref,
    state_ref, wide_ref, in_window_ref,
    normed_buf, out_buf,
):
    sec = place_ref[0]
    width = down_ref.shape[0]
    span = windows[1] * RANK
    own = pl.ds(pl.multiple_of(sec * windows[0], RANK), span)
    total = jnp.zeros((RANK, 1), F32)
    for k in range(4):
        patch = jnp.concatenate([image_ref[l, k] for l in range(sections)], axis=0).astype(F32)
        normed = (patch * norm_scale(patch)).astype(BF)
        normed_buf[...] = normed
        pre = dot_nn(normed, down_ref[...])
        act = gelu_tanh(pre).astype(BF)
        out = (patch + dot_nn(act, up_ref[...])).astype(BF)
        out_buf[k] = out
        out32 = out.astype(F32)
        total = total + jnp.sum(out32 * out32, axis=1, keepdims=True)
        state_ref[k] = gelu_slope(pre)
        state_ref[4 + k] = dot_nt(out, up_ref[...])
        wide_ref[:, k * RANK:(k + 1) * RANK] = act
        cross = dot(in_ref[k], up_ref[...], (0, 1))
        wide_ref[:, (4 + k) * RANK:(5 + k) * RANK] = cross.astype(BF)
        at = 8 * RANK + k * span
        wide_ref[:, at:at + span] = normed_buf[:, own]
        at += 4 * span
        wide_ref[:, at:at + span] = out_buf[k, :, own]
        in_window_ref[k * span:(k + 1) * span, :] = in_ref[k, own, :]
    scale = lax.rsqrt(total * (1.0 / (4 * width)) + EPS)
    proj = jnp.zeros((RANK, RANK), F32)
    for k in range(4):
        proj = proj + dot_nn((out_buf[k].astype(F32) * scale).astype(BF), in_ref[k])
    state_ref[8] = proj
    state_ref[9] = jnp.broadcast_to(scale, (RANK, RANK))
    per = sections // 4
    own = pl.ds(
        pl.multiple_of(lax.rem(sec, per) * in_windows[0], RANK), in_windows[1] * RANK
    )
    out = out_buf[sec // per, :, own].astype(F32)
    wide_ref[:, 8 * RANK + 8 * span:] = (out * scale).astype(BF)


def encoder_front(sec, images, enc_down, enc_up, proj_in):
    sections = images.shape[0]
    width = images.shape[3]
    windows = window(width, sections)
    in_windows = window(width, sections // 4)
    span = windows[1] * RANK
    total = 8 * RANK + 8 * span + in_windows[1] * RANK
    return pl.pallas_call(
        functools.partial(front_kernel, sections, windows, in_windows),
        in_specs=[SMEM] + [VMEM] * 4,
        out_specs=[VMEM] * 3,
        out_shape=[
            jax.ShapeDtypeStruct((10, RANK, RANK), F32),
            jax.ShapeDtypeStruct((RANK, total), BF),
            jax.ShapeDtypeStruct((4 * span, RANK), BF),
        ],
        scratch_shapes=[
            pltpu.VMEM((RANK, width), BF),
            pltpu.VMEM((4, RANK, width), BF),
        ],
        compiler_params=PARAMS,
    )(scalars(sec), images, enc_down, enc_up, proj_in)


def pack_kernel(layers, core_ref, gram_ref, out_ref, packed):
    at = 0
    for l in range(layers):
        size = (l + 2) * 16
        packed[at:at + size, :] = gram_ref[l, :size, :]
        at += size
    half = at // 2
    value = packed[pl.ds(pl.multiple_of(core_ref[0] * half, 16), half), :]
    for to in range(out_ref.shape[0]):
        out_ref[to] = value


def pack_gram(core, gram, groups):
    layers = gram.shape[0]
    total = sum((l + 2) * 16 for l in range(layers))
    return pl.pallas_call(
        functools.partial(pack_kernel, layers),
        in_specs=[SMEM, VMEM],
        out_specs=VMEM,
        out_shape=jax.ShapeDtypeStruct((groups, total // 2, RANK), BF),
        scratch_shapes=[pltpu.VMEM((total, RANK), BF)],
        compiler_params=PARAMS,
    )(scalars(core), gram)


def rank_kernel(
    layers, width,
    place_ref, own_ref, other_ref, gath_ref, state_ref, cot_ref, norm_ref, image_gram_ref, sel_ref,
    coef_ref, factor_ref, image_ref,
    weight, acts, act_cat, grads, scaled, back, pre_ref, slope_ref, inner_ref, scale_ref,
):
    rank = RANK
    own = place_ref[0]
    core = place_ref[1]
    at = 0
    for l in range(layers):
        for j in range(l + 2):
            which, place = divmod(at, own_ref.shape[1])
            span = slice(place, place + 16)
            tile = jnp.where(core == which, own_ref[:, span, :], other_ref[:, span, :])
            tile = tile.astype(F32)
            rows = slice(j * rank, (j + 1) * rank)
            weight[l, rows, :rank] = tile[:, :8, :].reshape(rank, rank).astype(BF)
            weight[l, rows, rank:] = tile[:, 8:, :].reshape(rank, rank).astype(BF)
            at += 16

    proj_pre = state_ref[8]
    sel = sel_ref[...]
    placed = dot_nn(sel, gelu_tanh(proj_pre).astype(BF))
    placed_half = placed.astype(BF)
    acts[0] = placed_half
    act_cat[:, :rank] = placed_half
    image_inner = dot_nn(placed_half, image_gram_ref[...])
    total = norm_ref[...] + jnp.sum(placed * image_inner, axis=1, keepdims=True)
    for l in range(layers):
        here = (l + 1) * rank
        scale = lax.rsqrt(jnp.maximum(total, 0.0) * (1.0 / width) + EPS)
        both = dot_nn(act_cat[:, :here], weight[l, :here, :])
        pre = scale * (gath_ref[l, :rank, :].astype(F32) + both[:, :rank])
        inner = gath_ref[l, rank:2 * rank, :].astype(F32) + both[:, rank:]
        sig = jax.nn.sigmoid(pre)
        act = (pre * sig).astype(BF)
        acts[l + 1] = act
        act_cat[:, here:here + rank] = act
        after = inner + dot_nn(act, weight[l, here:here + rank, rank:])
        total = total + jnp.sum(act.astype(F32) * (inner + after), axis=1, keepdims=True)
        pre_ref[l] = pre
        slope_ref[l] = sig * (1.0 + pre * (1.0 - sig))
        inner_ref[l] = after
        scale_ref[l] = scale
    back[...] = jnp.zeros_like(back)
    sums = jnp.zeros_like(total)
    for l in reversed(range(layers)):
        here = (l + 1) * rank
        cot = gath_ref[l, 2 * rank:3 * rank, :].astype(F32)
        d_act = cot - sums * inner_ref[l] + back[:, here:here + rank]
        d_pre = (d_act * slope_ref[l]).astype(BF).astype(F32)
        scale = scale_ref[l]
        mean = jnp.sum(d_pre * pre_ref[l], axis=1, keepdims=True) * (1.0 / width)
        grad = (scale * d_pre).astype(BF)
        part = (sums * acts[l + 1].astype(F32)).astype(BF)
        grads[l] = grad
        scaled[l + 1] = part
        pair = jnp.concatenate([grad, -part], axis=1)
        back[:, :here] += dot_nt(pair, weight[l, :here, :])
        sums = sums + scale * scale * mean
    d_image = cot_ref[...] - sums * image_inner + back[:, :rank]
    scaled[0] = (sums * placed).astype(BF)
    d_slot = dot_tn(sel, d_image.astype(BF))
    image_ref[0] = (d_slot * gelu_slope(proj_pre)).astype(BF)
    image_ref[1] = placed_half
    image_ref[2] = scaled[0]

    own_act = acts[own + 1]
    own_grad = grads[own]
    own_scaled = scaled[own + 1]
    factor_ref[0] = own_grad
    factor_ref[1] = own_act
    factor_ref[2] = own_scaled
    coef_ref[0] = dot_tn(acts[0], own_grad).astype(BF)
    for l in range(layers):
        low = l < own
        left = jnp.where(low, acts[l + 1], grads[l])
        right = jnp.where(low, own_grad, own_act)
        coef_ref[l + 1] = dot_tn(left, right).astype(BF)
    for l in range(layers + 1):
        low = l <= own + 1
        left = jnp.where(low, acts[l], scaled[l])
        right = jnp.where(low, own_scaled, own_act)
        coef_ref[layers + 1 + l] = dot_tn(left, right).astype(BF)


def rank_space(position, core, gram, other, gath, state, cot, norms, image_gram, sel, width):
    layers = gath.shape[0]
    rank = RANK
    tall = (layers + 1) * rank
    return pl.pallas_call(
        functools.partial(rank_kernel, layers, width),
        in_specs=[SMEM] + [VMEM] * 8,
        out_specs=[VMEM] * 3,
        out_shape=[
            jax.ShapeDtypeStruct((2 * layers + 2, rank, rank), BF),
            jax.ShapeDtypeStruct((3, rank, rank), BF),
            jax.ShapeDtypeStruct((3, rank, rank), BF),
        ],
        scratch_shapes=[
            pltpu.VMEM((layers, tall, 2 * rank), BF),
            pltpu.VMEM((layers + 1, rank, rank), BF),
            pltpu.VMEM((rank, tall), BF),
            pltpu.VMEM((layers, rank, rank), BF),
            pltpu.VMEM((layers + 1, rank, rank), BF),
            pltpu.VMEM((rank, tall), F32),
            pltpu.VMEM((layers, rank, rank), F32),
            pltpu.VMEM((layers, rank, rank), F32),
            pltpu.VMEM((layers, rank, rank), F32),
            pltpu.VMEM((layers, rank, 1), F32),
        ],
        compiler_params=PARAMS,
    )(scalars(position, core), gram, other, gath, state, cot, norms, image_gram, sel)


def late_kernel(
    enc_width, tiles, in_tiles, pieces,
    shift_ref, image_ref, state_ref, wide_ref, in_ref, block_ref,
    part_ref,
    down, up, proj, last,
):
    span = tiles * RANK
    d_proj = image_ref[0]
    placed = image_ref[1]
    d_proj32 = d_proj.astype(F32)
    proj_scale = state_ref[9]
    mean = jnp.sum(d_proj32 * state_ref[8], axis=1, keepdims=True) * (1.0 / (4 * enc_width))
    d_scaled = (d_proj32 * proj_scale).astype(BF)
    pull = mean * proj_scale * proj_scale
    total_down = jnp.zeros((span, RANK), F32)
    total_up = jnp.zeros((span, RANK), F32)
    for k in range(4):
        act = wide_ref[:, k * RANK:(k + 1) * RANK]
        cross = wide_ref[:, (4 + k) * RANK:(5 + k) * RANK]
        at = 8 * RANK + k * span
        normed = wide_ref[:, at:at + span]
        at += 4 * span
        out = wide_ref[:, at:at + span]
        d_enc = (dot_nn(d_scaled, cross) - pull * state_ref[4 + k]) * state_ref[k]
        total_down += dot_tn(normed, d_enc.astype(BF))
        inner = dot_tn(d_scaled, act).astype(BF)
        total_up += dot_nn(in_ref[k * span:(k + 1) * span, :], inner)
        total_up -= dot_tn(out, (pull * act.astype(F32)).astype(BF))
    down[:span, :] = total_down
    up[:span, :] = total_up
    proj[:in_tiles * RANK, :] = dot_tn(wide_ref[:, 8 * RANK + 8 * span:], d_proj)
    last[...] = dot_tn(block_ref[0], placed) - dot_tn(
        block_ref[1], dot_tn(placed, image_ref[2]).astype(BF)
    )
    groups = part_ref.shape[0]
    n_enc, n_in, pad_enc, pad_in = pieces
    n_out = last.shape[0] // groups
    for to in range(groups):
        at = shift_ref[0] + n_enc * to
        part_ref[to, :pad_enc, :] = down[pl.ds(at, pad_enc), :].astype(BF)
        part_ref[to, pad_enc:2 * pad_enc, :] = up[pl.ds(at, pad_enc), :].astype(BF)
        at = shift_ref[1] + n_in * to
        part_ref[to, 2 * pad_enc:2 * pad_enc + pad_in, :] = proj[pl.ds(at, pad_in), :].astype(BF)
        part_ref[to, 2 * pad_enc + pad_in:, :] = last[to * n_out:(to + 1) * n_out, :].astype(BF)


def encoder_late(sec, image, state, wide, in_window, blocks, enc_width, sections, groups):
    tiles = window(enc_width, sections)[1]
    in_tiles = window(enc_width, sections // 4)[1]
    block = enc_width // sections
    in_block = 4 * block
    n_enc = block // groups
    n_in = in_block // groups
    pad_enc = -(-n_enc // 16) * 16
    pad_in = -(-n_in // 16) * 16
    shifts = scalars(
        sec * (block % RANK), (sec % (sections // 4)) * (in_block % RANK)
    )
    columns = blocks.shape[2]
    total = 2 * pad_enc + pad_in + columns // groups
    pieces = (n_enc, n_in, pad_enc, pad_in)
    parts = pl.pallas_call(
        functools.partial(late_kernel, enc_width, tiles, in_tiles, pieces),
        in_specs=[SMEM] + [VMEM] * 5,
        out_specs=VMEM,
        out_shape=jax.ShapeDtypeStruct((groups, total, RANK), BF),
        scratch_shapes=[
            pltpu.VMEM((tiles * RANK + 16, RANK), F32),
            pltpu.VMEM((tiles * RANK + 16, RANK), F32),
            pltpu.VMEM((in_tiles * RANK + 16, RANK), F32),
            pltpu.VMEM((columns, RANK), F32),
        ],
        compiler_params=PARAMS,
    )(shifts, image, state, wide, in_window, blocks)
    return parts, pieces


def last_kernel(
    layers,
    place_ref, text_ref, cot_ref, other_text_ref, other_cot_ref,
    factor_ref, mixed_ref, slice_ref, out_ref,
    grad_down_ref, grad_up_ref,
    coef,
):
    sec = place_ref[0]
    core = place_ref[1]
    groups, half, share = text_ref.shape
    chunk = coef.shape[0] // groups
    for at in range(groups):
        coef[at * chunk:(at + 1) * chunk, :] = mixed_ref[at, :chunk, :]

    def block(index):
        return coef[index * RANK:(index + 1) * RANK, :]

    def flat(value):
        return value.reshape(groups * half, value.shape[-1])

    total_down = jnp.zeros((share, RANK), F32)
    total_up = jnp.zeros((RANK, share), F32)
    for first, second, which in (
        (text_ref, cot_ref, core), (other_text_ref, other_cot_ref, 1 - core)
    ):
        span = pl.ds(pl.multiple_of(which * half, half), half)
        text = flat(first[...])
        total_down += dot_tn(text, flat(factor_ref[:, 0, span, :]))
        total_up += dot_tn(flat(factor_ref[:, 1, span, :]), flat(second[...]))
        total_up -= dot_tn(flat(factor_ref[:, 2, span, :]), text)
    total_down += dot_tn(out_ref[...], block(0))
    total_up -= dot_tn(block(layers + 1), out_ref[...])
    turned = jnp.zeros((share, RANK), F32)
    for l in range(layers):
        pair = block(l + 1)
        zero = jnp.zeros_like(pair)
        up = jnp.concatenate(
            [
                slice_ref[l, share + m * RANK:share + (m + 1) * RANK, :]
                for m in range(share // RANK)
            ],
            axis=1,
        )
        total_down += dot_tn(up, jnp.where(l < sec, pair, zero))
        turned += dot_nn(slice_ref[l, :share, :], jnp.where(l > sec, pair, zero))
        total_up -= dot_tn(block(layers + 2 + l), up)
    grad_down_ref[...] = total_down
    grad_up_ref[...] = total_up + turned.T


def last_products(sec, own, other, factors, mixed, slices, out):
    layers = slices.shape[0]
    share = out.shape[1]
    return pl.pallas_call(
        functools.partial(last_kernel, layers),
        in_specs=[SMEM] + [VMEM] * 8,
        out_specs=[VMEM] * 2,
        out_shape=[
            jax.ShapeDtypeStruct((share, RANK), F32),
            jax.ShapeDtypeStruct((RANK, share), F32),
        ],
        scratch_shapes=[pltpu.VMEM(((2 * layers + 2) * RANK, RANK), BF)],
        compiler_params=PARAMS,
    )(scalars(sec, sec % 2), *own, *other, factors, mixed, slices, out)


def spread(value, axis):
    count = lax.axis_size(axis)
    return lax.all_to_all(jnp.broadcast_to(value[None], (count,) + value.shape), axis, 0, 0)


def shards(text, cotangent, dec_down, dec_up, images, enc_down, enc_up, proj_in, proj_out, frame):
    sections = lax.axis_size("section")
    groups = lax.axis_size("dp")
    sec = lax.axis_index("section")
    grp = lax.axis_index("dp")
    core = sec % 2
    slot_count, patch_count, enc_width = images.shape[2:]
    tokens = patch_count // 4
    rows_total, width = text.shape[1:]
    rank = dec_down.shape[2]
    weight_down = dec_down[0]
    weight_up = dec_up[0]
    frames = frame[0]
    text = text[0]
    cot = cotangent[0]
    piece = rank // groups
    swap = [(at, at ^ 1) for at in range(sections)]

    up_rows = lax.all_gather(
        lax.dynamic_slice_in_dim(weight_up, grp * piece, piece, 0), "section", axis=0
    )

    slot_row = jnp.repeat(frames, tokens)[None, :]
    row = jnp.arange(rows_total, dtype=jnp.int32)[:, None]
    column = jnp.arange(rows_total, dtype=jnp.int32)[None, :]
    sel = (slot_row == row // tokens) & (row % tokens == column % tokens)
    keep = 1.0 - jnp.any(sel, axis=1, keepdims=True).astype(F32)
    sel = sel.astype(BF)
    text_cols, cot_cols, proj, cot_image, text_norm, image_gram, picks, blocks, own_slices, out_slice = (
        text_products(
            sec, grp, keep, text, cot, weight_down, weight_up, proj_out, sections, groups
        )
    )
    text_cols = lax.all_to_all(text_cols, "dp", 0, 0)
    own_images = images[0, 0].reshape(slot_count * tokens, 4, enc_width).transpose(1, 0, 2)

    image_rows = lax.dynamic_slice_in_dim(proj_out, grp * piece, piece, 0)
    up_rows, text_cols, cot_cols, own_images, image_rows = lax.optimization_barrier(
        (up_rows, text_cols, cot_cols, own_images, image_rows)
    )
    cot_cols = lax.all_to_all(cot_cols, "dp", 0, 0)
    group_images = lax.all_gather(own_images, "section", axis=0)
    rows = jnp.concatenate([image_rows[None], up_rows], axis=0).reshape(-1, width)
    gram = jnp.stack(
        [
            dot_nn(rows, weight_down).reshape(sections + 1, piece, rank),
            dot_nt(rows, weight_up).reshape(sections + 1, piece, rank),
        ],
        axis=1,
    ).astype(BF).reshape(-1, rank)
    packed = pack_gram(core, lax.all_gather(gram, "section", axis=0), groups)
    packed, cot_cols, proj = lax.optimization_barrier((packed, cot_cols, proj))
    own_gram = lax.all_to_all(packed, "dp", 0, 0)

    gath = lax.all_gather(proj, "section", axis=0)
    quarters = proj_in.reshape(4, enc_width, rank)
    state, wide, in_window = encoder_front(sec, group_images, enc_down, enc_up, quarters)
    own_gram, gath, state, wide, in_window = lax.optimization_barrier(
        (own_gram, gath, state, wide, in_window)
    )
    other_gram = lax.ppermute(own_gram, "section", swap)
    own_cols = (text_cols, cot_cols)
    other_cols = tuple(lax.ppermute(cols, "section", swap) for cols in own_cols)
    own_slices, state = lax.optimization_barrier((own_slices, state))
    slices = lax.all_gather(own_slices, "section", axis=0)

    coef, factor, image = rank_space(
        sec, core, own_gram, other_gram, gath, state, cot_image, text_norm, image_gram, sel, width
    )
    coef = lax.all_to_all(coef.reshape(groups, -1, rank), "dp", 0, 0)
    factors = lax.all_gather(factor, "dp", axis=0)

    parts, (n_enc, n_in, pad_enc, pad_in) = encoder_late(
        sec, image, state, wide, in_window, blocks, enc_width, sections, groups
    )
    coef = jnp.sum(coef.astype(F32), axis=0).astype(BF)
    chunk = coef.shape[0]
    mixed = jnp.concatenate(
        [jnp.broadcast_to(coef[None], (groups,) + coef.shape), parts], axis=1
    )
    mixed = lax.all_to_all(mixed, "dp", 0, 0)

    first_coef = mixed[0, :rank]
    at = (sections + 1) * rank
    last_coef = mixed[at // chunk, at % chunk:at % chunk + rank]
    few = picks.shape[2]
    term = dot_nt(picks[:, 0].reshape(-1, rank), first_coef)
    term = term - dot_nt(picks[:, 1].reshape(-1, rank), last_coef)
    term = lax.all_to_all(term.astype(BF).reshape(sections, few, rank), "section", 0, 0)

    grad_dec_down, grad_dec_up = last_products(
        sec, own_cols, other_cols, factors, mixed, slices, out_slice
    )
    parts = jnp.sum(mixed[:, chunk:].astype(F32), axis=0)
    grad_enc_down = parts[:n_enc]
    grad_enc_up = parts[pad_enc:pad_enc + n_enc].T
    grad_proj_in = parts[2 * pad_enc:2 * pad_enc + n_in]
    own_out = parts[2 * pad_enc + pad_in:]
    grad_proj_out = (own_out + jnp.sum(term.astype(F32), axis=0)).T
    return (
        grad_dec_down[None],
        grad_dec_up[None],
        grad_enc_down,
        grad_enc_up,
        grad_proj_in,
        grad_proj_out,
    )


def solution(mesh):
    placed = (
        P("dp", None, None),
        P("dp", None, None),
        P("section", None, None),
        P("section", None, None),
        P("dp", "section", None, None, None),
        P(),
        P(),
        P(),
        P(),
        P("dp", None),
    )
    return jax.shard_map(
        shards,
        mesh=mesh,
        in_specs=placed,
        out_specs=(
            P("section", "dp", None),
            P("section", None, "dp"),
            P(("section", "dp"), None),
            P(None, ("section", "dp")),
            P(("section", "dp"), None),
            P(None, ("section", "dp")),
        ),
        check_vma=False,
    )
```

```python
import functools

import jax
import jax.numpy as jnp
from jax import lax
from jax.experimental import pallas as pl
from jax.experimental.pallas import tpu as pltpu
from jax.sharding import PartitionSpec as P

EPS = 1e-06
GELU_C = 0.7978845608028654
BF = jnp.bfloat16
F32 = jnp.float32


def gelu_tanh(value):
    return 0.5 * value * (1.0 + jnp.tanh(GELU_C * (value + 0.044715 * value * value * value)))


def gelu_slope(value):
    inner = jnp.tanh(GELU_C * (value + 0.044715 * value * value * value))
    return 0.5 * (1.0 + inner) + 0.5 * value * (1.0 - inner * inner) * GELU_C * (
        1.0 + 3.0 * 0.044715 * value * value
    )


def norm_scale(rows32):
    return lax.rsqrt(jnp.mean(rows32 * rows32, axis=-1, keepdims=True) + EPS)


def dot(left, right, dims):
    return lax.dot_general(left, right, ((dims[:1], dims[1:]), ((), ())), preferred_element_type=F32)


def dot_nn(left, right):
    return dot(left, right, (1, 0))


def dot_tn(left, right):
    return dot(left, right, (0, 0))


def dot_nt(left, right):
    return dot(left, right, (1, 1))


RANK = 128
VMEM = pl.BlockSpec(memory_space=pltpu.VMEM)
SMEM = pl.BlockSpec(memory_space=pltpu.SMEM)
PARAMS = pltpu.CompilerParams(vmem_limit_bytes=48 * 1024 * 1024)


def scalars(*values):
    return jnp.stack(values).astype(jnp.int32)


def text_kernel(
    part, share, few, steps,
    place_ref, keep_ref, text_ref, cot_ref, down_ref, up_ref, out_ref,
    cols_ref, proj_ref, image_ref, norm_ref, gram_ref,
    pick_ref, block_ref, slice_ref, out_slice_ref,
    proj, image, gram,
):
    step = pl.program_id(0)
    sec, grp = place_ref[0], place_ref[1]

    @pl.when(step == 0)
    def _():
        proj[...] = jnp.zeros_like(proj)
        image[...] = jnp.zeros_like(image)
        gram[...] = jnp.zeros_like(gram)
        norm_ref[...] = jnp.zeros_like(norm_ref)

    text32 = text_ref[...].astype(F32) * keep_ref[...]
    text = text32.astype(BF)
    cot = cot_ref[...]
    norm_ref[...] += jnp.sum(text32 * text32, axis=1, keepdims=True)
    proj[:RANK] += dot_nn(text, down_ref[...])
    proj[RANK:2 * RANK] += dot_nt(text, up_ref[...])
    proj[2 * RANK:] += dot_nt(cot, up_ref[...])
    image[...] += dot_nt(cot, out_ref[...])
    gram[...] += dot_nt(out_ref[...], out_ref[...])

    own = pl.ds(pl.multiple_of(lax.rem(sec, 4) * part, part), part)
    keep = keep_ref[own, :]
    pieces = cols_ref.shape[0]
    for piece in range(pieces):
        span = slice(piece * share, (piece + 1) * share)
        cols_ref[piece, :part, :] = (text_ref[own, span].astype(F32) * keep).astype(BF)
        cols_ref[piece, part:, :] = cot_ref[own, span]

    pick_ref[0, 0] = down_ref[pl.ds(pl.multiple_of(grp * few, few), few), :]
    per = RANK // few
    lanes = up_ref[:, pl.ds(pl.multiple_of(grp // per * RANK, RANK), RANK)].astype(F32).T
    picked = lanes[:few]
    for at in range(1, per):
        picked = jnp.where(lax.rem(grp, per) == at, lanes[at * few:(at + 1) * few], picked)
    pick_ref[0, 1] = picked.astype(BF)

    @pl.when(step == sec)
    def _():
        block_ref[0] = cot
        block_ref[1] = out_ref[...]

    @pl.when(step == grp // pieces)
    def _():
        at = pl.multiple_of(lax.rem(grp, pieces) * share, share)
        slice_ref[:share, :] = down_ref[pl.ds(at, share), :]
        up = up_ref[:, pl.ds(at, share)]
        for m in range(share // RANK):
            slice_ref[share + m * RANK:share + (m + 1) * RANK, :] = up[:, m * RANK:(m + 1) * RANK]
        out_slice_ref[...] = out_ref[:, pl.ds(at, share)]

    @pl.when(step == steps - 1)
    def _():
        proj_ref[...] = proj[...].astype(BF)
        image_ref[...] = image[...]
        gram_ref[...] = gram[...].astype(BF)


def text_products(sec, grp, keep, text, cot, down, up, out, sections, groups):
    rows, width = text.shape
    share = width // groups
    steps = sections
    wide = width // steps
    pieces = wide // share
    few = wide // groups
    part = rows // 4
    across = pl.BlockSpec((rows, wide), lambda i: (0, i))
    fixed = pl.BlockSpec((rows, RANK), lambda i: (0, 0))
    column = pl.BlockSpec((rows, 1), lambda i: (0, 0))
    return pl.pallas_call(
        functools.partial(text_kernel, part, share, few, steps),
        grid=(steps,),
        in_specs=[
            SMEM,
            column,
            across,
            across,
            pl.BlockSpec((wide, RANK), lambda i: (i, 0)),
            across,
            across,
        ],
        out_specs=[
            pl.BlockSpec((pieces, 2 * part, share), lambda i: (i, 0, 0)),
            pl.BlockSpec((3 * RANK, RANK), lambda i: (0, 0)),
            fixed,
            column,
            fixed,
            pl.BlockSpec((1, 2, few, RANK), lambda i: (i, 0, 0, 0)),
            pl.BlockSpec((2, rows, wide), lambda i: (0, 0, 0)),
            pl.BlockSpec((2 * share, RANK), lambda i: (0, 0)),
            pl.BlockSpec((rows, share), lambda i: (0, 0)),
        ],
        out_shape=[
            jax.ShapeDtypeStruct((groups, 2 * part, share), BF),
            jax.ShapeDtypeStruct((3 * RANK, RANK), BF),
            jax.ShapeDtypeStruct((rows, RANK), F32),
            jax.ShapeDtypeStruct((rows, 1), F32),
            jax.ShapeDtypeStruct((RANK, RANK), BF),
            jax.ShapeDtypeStruct((steps, 2, few, RANK), BF),
            jax.ShapeDtypeStruct((2, rows, wide), BF),
            jax.ShapeDtypeStruct((2 * share, RANK), BF),
            jax.ShapeDtypeStruct((rows, share), BF),
        ],
        scratch_shapes=[
            pltpu.VMEM((3 * RANK, RANK), F32),
            pltpu.VMEM((rows, RANK), F32),
            pltpu.VMEM((RANK, RANK), F32),
        ],
        compiler_params=PARAMS,
    )(scalars(sec, grp), keep, text, cot, down, up, out)


def window(width, count):
    block = width // count
    stride = block // RANK * RANK
    tiles = -(-((count - 1) * (block - stride) + block) // RANK)
    return stride, tiles


def front_kernel(
    sections, windows, in_windows,
    place_ref, image_ref, down_ref, up_ref, in_ref,
    state_ref, wide_ref, in_window_ref,
    normed_buf, out_buf,
):
    sec = place_ref[0]
    width = down_ref.shape[0]
    span = windows[1] * RANK
    own = pl.ds(pl.multiple_of(sec * windows[0], RANK), span)
    total = jnp.zeros((RANK, 1), F32)
    for k in range(4):
        patch = jnp.concatenate([image_ref[l, k] for l in range(sections)], axis=0).astype(F32)
        normed = (patch * norm_scale(patch)).astype(BF)
        normed_buf[...] = normed
        pre = dot_nn(normed, down_ref[...])
        act = gelu_tanh(pre).astype(BF)
        out = (patch + dot_nn(act, up_ref[...])).astype(BF)
        out_buf[k] = out
        out32 = out.astype(F32)
        total = total + jnp.sum(out32 * out32, axis=1, keepdims=True)
        state_ref[k] = gelu_slope(pre)
        state_ref[4 + k] = dot_nt(out, up_ref[...])
        wide_ref[:, k * RANK:(k + 1) * RANK] = act
        cross = dot(in_ref[k], up_ref[...], (0, 1))
        wide_ref[:, (4 + k) * RANK:(5 + k) * RANK] = cross.astype(BF)
        at = 8 * RANK + k * span
        wide_ref[:, at:at + span] = normed_buf[:, own]
        at += 4 * span
        wide_ref[:, at:at + span] = out_buf[k, :, own]
        in_window_ref[k * span:(k + 1) * span, :] = in_ref[k, own, :]
    scale = lax.rsqrt(total * (1.0 / (4 * width)) + EPS)
    proj = jnp.zeros((RANK, RANK), F32)
    for k in range(4):
        proj = proj + dot_nn((out_buf[k].astype(F32) * scale).astype(BF), in_ref[k])
    state_ref[8] = proj
    state_ref[9] = jnp.broadcast_to(scale, (RANK, RANK))
    per = sections // 4
    own = pl.ds(
        pl.multiple_of(lax.rem(sec, per) * in_windows[0], RANK), in_windows[1] * RANK
    )
    out = out_buf[sec // per, :, own].astype(F32)
    wide_ref[:, 8 * RANK + 8 * span:] = (out * scale).astype(BF)


def encoder_front(sec, images, enc_down, enc_up, proj_in):
    sections = images.shape[0]
    width = images.shape[3]
    windows = window(width, sections)
    in_windows = window(width, sections // 4)
    span = windows[1] * RANK
    total = 8 * RANK + 8 * span + in_windows[1] * RANK
    return pl.pallas_call(
        functools.partial(front_kernel, sections, windows, in_windows),
        in_specs=[SMEM] + [VMEM] * 4,
        out_specs=[VMEM] * 3,
        out_shape=[
            jax.ShapeDtypeStruct((10, RANK, RANK), F32),
            jax.ShapeDtypeStruct((RANK, total), BF),
            jax.ShapeDtypeStruct((4 * span, RANK), BF),
        ],
        scratch_shapes=[
            pltpu.VMEM((RANK, width), BF),
            pltpu.VMEM((4, RANK, width), BF),
        ],
        compiler_params=PARAMS,
    )(scalars(sec), images, enc_down, enc_up, proj_in)


def two_lanes(column):
    high = column.astype(BF).astype(F32)
    lane = lax.broadcasted_iota(jnp.int32, (column.shape[0], RANK), 1)
    zero = jnp.zeros((column.shape[0], RANK), F32)
    return jnp.where(lane == 0, high, jnp.where(lane == 1, column - high, zero))


def pack_kernel(layers, core_ref, gram_ref, out_ref, packed):
    at = 0
    for l in range(layers):
        size = (l + 2) * 16
        packed[at:at + size, :] = gram_ref[l, :size, :]
        at += size
    half = at // 2
    value = packed[pl.ds(pl.multiple_of(core_ref[0] * half, 16), half), :]
    for to in range(out_ref.shape[0]):
        out_ref[to] = value


def pack_gram(core, gram, groups):
    layers = gram.shape[0]
    total = sum((l + 2) * 16 for l in range(layers))
    return pl.pallas_call(
        functools.partial(pack_kernel, layers),
        in_specs=[SMEM, VMEM],
        out_specs=VMEM,
        out_shape=jax.ShapeDtypeStruct((groups, total // 2, RANK), BF),
        scratch_shapes=[pltpu.VMEM((total, RANK), BF)],
        compiler_params=PARAMS,
    )(scalars(core), gram)


def rank_kernel(
    layers, width,
    place_ref, own_ref, other_ref, gath_ref, state_ref, cot_ref, norm_ref, image_gram_ref, sel_ref,
    coef_ref, factor_ref, image_ref,
    weight, acts, act_cat, grads, scaled, back, pre_ref, slope_ref, inner_ref, scale_ref, sums_ref,
):
    rank = RANK
    own = place_ref[0]
    core = place_ref[1]
    at = 0
    for l in range(layers):
        for j in range(l + 2):
            which, place = divmod(at, own_ref.shape[1])
            span = slice(place, place + 16)
            tile = jnp.where(core == which, own_ref[:, span, :], other_ref[:, span, :])
            tile = tile.astype(F32)
            rows = slice(j * rank, (j + 1) * rank)
            weight[l, rows, :rank] = tile[:, :8, :].reshape(rank, rank).astype(BF)
            weight[l, rows, rank:] = tile[:, 8:, :].reshape(rank, rank).astype(BF)
            at += 16

    proj_pre = state_ref[8]
    sel = sel_ref[...]
    placed = dot_nn(sel, gelu_tanh(proj_pre).astype(BF))
    placed_half = placed.astype(BF)
    acts[0] = placed_half
    act_cat[:, :rank] = placed_half
    image_inner = dot_nn(placed_half, image_gram_ref[...])
    total = norm_ref[...] + jnp.sum(placed * image_inner, axis=1, keepdims=True)
    for l in range(layers):
        here = (l + 1) * rank
        scale = lax.rsqrt(jnp.maximum(total, 0.0) * (1.0 / width) + EPS)
        both = dot_nn(act_cat[:, :here], weight[l, :here, :])
        pre = scale * (gath_ref[l, :rank, :].astype(F32) + both[:, :rank])
        inner = gath_ref[l, rank:2 * rank, :].astype(F32) + both[:, rank:]
        sig = jax.nn.sigmoid(pre)
        act = (pre * sig).astype(BF)
        acts[l + 1] = act
        act_cat[:, here:here + rank] = act
        after = inner + dot_nn(act, weight[l, here:here + rank, rank:])
        total = total + jnp.sum(act.astype(F32) * (inner + after), axis=1, keepdims=True)
        pre_ref[l] = pre
        slope_ref[l] = sig * (1.0 + pre * (1.0 - sig))
        inner_ref[l] = after
        scale_ref[l] = scale
    back[...] = jnp.zeros_like(back)
    sums = jnp.zeros_like(total)
    for l in reversed(range(layers)):
        here = (l + 1) * rank
        cot = gath_ref[l, 2 * rank:3 * rank, :].astype(F32)
        d_act = cot - sums * inner_ref[l] + back[:, here:here + rank]
        d_pre = (d_act * slope_ref[l]).astype(BF).astype(F32)
        scale = scale_ref[l]
        mean = jnp.sum(d_pre * pre_ref[l], axis=1, keepdims=True) * (1.0 / width)
        grad = (scale * d_pre).astype(BF)
        part = (sums * acts[l + 1].astype(F32)).astype(BF)
        grads[l] = grad
        scaled[l + 1] = part
        sums_ref[l] = sums
        pair = jnp.concatenate([grad, -part], axis=1)
        back[:, :here] += dot_nt(pair, weight[l, :here, :])
        sums = sums + scale * scale * mean
    d_image = cot_ref[...] - sums * image_inner + back[:, :rank]
    scaled[0] = (sums * placed).astype(BF)
    d_slot = dot_tn(sel, d_image.astype(BF))
    image_ref[0] = (d_slot * gelu_slope(proj_pre)).astype(BF)
    image_ref[1] = placed_half
    image_ref[2] = scaled[0]

    own_act = acts[own + 1]
    own_grad = grads[own]
    own_scaled = scaled[own + 1]
    factor_ref[:rank, :] = own_grad
    factor_ref[rank:2 * rank, :] = own_act
    factor_ref[2 * rank:, :] = two_lanes(sums_ref[own]).T[:16].astype(BF)
    coef_ref[0] = dot_tn(acts[0], own_grad).astype(BF)
    for l in range(layers):
        low = l < own
        left = jnp.where(low, acts[l + 1], grads[l])
        right = jnp.where(low, own_grad, own_act)
        coef_ref[l + 1] = dot_tn(left, right).astype(BF)
    for l in range(layers + 1):
        low = l <= own + 1
        left = jnp.where(low, acts[l], scaled[l])
        right = jnp.where(low, own_scaled, own_act)
        coef_ref[layers + 1 + l] = dot_tn(left, right).astype(BF)


def rank_space(position, core, gram, other, gath, state, cot, norms, image_gram, sel, width):
    layers = gath.shape[0]
    rank = RANK
    tall = (layers + 1) * rank
    operands = (gram, other, gath, state, cot, norms, image_gram, sel)

    def whole(shape):
        return pl.BlockSpec(shape, lambda i: (0,) * len(shape))

    outs = ((2 * layers + 2, rank, rank), (2 * rank + 16, rank), (3, rank, rank))
    return pl.pallas_call(
        functools.partial(rank_kernel, layers, width),
        grid=(1,),
        in_specs=[SMEM] + [whole(value.shape) for value in operands],
        out_specs=[whole(shape) for shape in outs],
        out_shape=[jax.ShapeDtypeStruct(shape, BF) for shape in outs],
        scratch_shapes=[
            pltpu.VMEM((layers, tall, 2 * rank), BF),
            pltpu.VMEM((layers + 1, rank, rank), BF),
            pltpu.VMEM((rank, tall), BF),
            pltpu.VMEM((layers, rank, rank), BF),
            pltpu.VMEM((layers + 1, rank, rank), BF),
            pltpu.VMEM((rank, tall), F32),
            pltpu.VMEM((layers, rank, rank), F32),
            pltpu.VMEM((layers, rank, rank), F32),
            pltpu.VMEM((layers, rank, rank), F32),
            pltpu.VMEM((layers, rank, 1), F32),
            pltpu.VMEM((layers, rank, 1), F32),
        ],
        compiler_params=PARAMS,
    )(scalars(position, core), *operands)


def late_kernel(
    enc_width, tiles, in_tiles, pieces,
    shift_ref, image_ref, state_ref, wide_ref, in_ref, block_ref,
    part_ref,
    down, up, proj, last,
):
    span = tiles * RANK
    d_proj = image_ref[0]
    placed = image_ref[1]
    d_proj32 = d_proj.astype(F32)
    proj_scale = state_ref[9]
    mean = jnp.sum(d_proj32 * state_ref[8], axis=1, keepdims=True) * (1.0 / (4 * enc_width))
    d_scaled = (d_proj32 * proj_scale).astype(BF)
    pull = mean * proj_scale * proj_scale
    total_down = jnp.zeros((span, RANK), F32)
    total_up = jnp.zeros((span, RANK), F32)
    for k in range(4):
        act = wide_ref[:, k * RANK:(k + 1) * RANK]
        cross = wide_ref[:, (4 + k) * RANK:(5 + k) * RANK]
        at = 8 * RANK + k * span
        normed = wide_ref[:, at:at + span]
        at += 4 * span
        out = wide_ref[:, at:at + span]
        d_enc = (dot_nn(d_scaled, cross) - pull * state_ref[4 + k]) * state_ref[k]
        total_down += dot_tn(normed, d_enc.astype(BF))
        inner = dot_tn(d_scaled, act).astype(BF)
        total_up += dot_nn(in_ref[k * span:(k + 1) * span, :], inner)
        total_up -= dot_tn(out, (pull * act.astype(F32)).astype(BF))
    down[:span, :] = total_down
    up[:span, :] = total_up
    proj[:in_tiles * RANK, :] = dot_tn(wide_ref[:, 8 * RANK + 8 * span:], d_proj)
    last[...] = dot_tn(block_ref[0], placed) - dot_tn(
        block_ref[1], dot_tn(placed, image_ref[2]).astype(BF)
    )
    groups = part_ref.shape[0]
    n_enc, n_in, pad_enc, pad_in = pieces
    n_out = last.shape[0] // groups
    for to in range(groups):
        at = shift_ref[0] + n_enc * to
        part_ref[to, :pad_enc, :] = down[pl.ds(at, pad_enc), :].astype(BF)
        part_ref[to, pad_enc:2 * pad_enc, :] = up[pl.ds(at, pad_enc), :].astype(BF)
        at = shift_ref[1] + n_in * to
        part_ref[to, 2 * pad_enc:2 * pad_enc + pad_in, :] = proj[pl.ds(at, pad_in), :].astype(BF)
        part_ref[to, 2 * pad_enc + pad_in:, :] = last[to * n_out:(to + 1) * n_out, :].astype(BF)


def encoder_late(sec, image, state, wide, in_window, blocks, enc_width, sections, groups):
    tiles = window(enc_width, sections)[1]
    in_tiles = window(enc_width, sections // 4)[1]
    block = enc_width // sections
    in_block = 4 * block
    n_enc = block // groups
    n_in = in_block // groups
    pad_enc = -(-n_enc // 16) * 16
    pad_in = -(-n_in // 16) * 16
    shifts = scalars(
        sec * (block % RANK), (sec % (sections // 4)) * (in_block % RANK)
    )
    columns = blocks.shape[2]
    total = 2 * pad_enc + pad_in + columns // groups
    pieces = (n_enc, n_in, pad_enc, pad_in)
    parts = pl.pallas_call(
        functools.partial(late_kernel, enc_width, tiles, in_tiles, pieces),
        in_specs=[SMEM] + [VMEM] * 5,
        out_specs=VMEM,
        out_shape=jax.ShapeDtypeStruct((groups, total, RANK), BF),
        scratch_shapes=[
            pltpu.VMEM((tiles * RANK + 16, RANK), F32),
            pltpu.VMEM((tiles * RANK + 16, RANK), F32),
            pltpu.VMEM((in_tiles * RANK + 16, RANK), F32),
            pltpu.VMEM((columns, RANK), F32),
        ],
        compiler_params=PARAMS,
    )(shifts, image, state, wide, in_window, blocks)
    return parts, pieces


def row_kernel(
    place_ref, first_ref, second_ref, third_ref, fourth_ref, factor_ref,
    down_ref, up_ref,
    acts, scaled,
):
    groups, rows, share = first_ref.shape
    part = rows // 2
    for at in range(groups):
        act = factor_ref[at, RANK:2 * RANK, :]
        weights = factor_ref[at, 2 * RANK:2 * RANK + 8, :].astype(F32)
        weights = jnp.sum(weights, axis=0, keepdims=True)
        weights = jnp.broadcast_to(weights, (RANK, RANK)).T
        acts[at] = act
        scaled[at] = (act.astype(F32) * weights).astype(BF)

    def flat(value):
        return value.reshape(groups * part, value.shape[-1])

    total_down = jnp.zeros((share, RANK), F32)
    total_up = jnp.zeros((RANK, share), F32)
    own = place_ref[0]
    for at, cols_ref in enumerate((first_ref, second_ref, third_ref, fourth_ref)):
        which = lax.rem(own, 2) if at % 2 == 0 else 1 - lax.rem(own, 2)
        which = which + 2 * (own // 2 if at < 2 else 1 - own // 2)
        start = pl.multiple_of(which * part, part)
        text = flat(cols_ref[:, :part, :])
        cot = flat(cols_ref[:, part:, :])
        total_down += dot_tn(text, flat(factor_ref[:, pl.ds(start, part), :]))
        total_up += dot_tn(flat(acts[:, pl.ds(start, part), :]), cot)
        total_up -= dot_tn(flat(scaled[:, pl.ds(start, part), :]), text)
    down_ref[...] = total_down
    up_ref[...] = total_up


def row_products(sec, cols, factors):
    groups, _, share = cols[0].shape
    return pl.pallas_call(
        row_kernel,
        in_specs=[SMEM] + [VMEM] * 5,
        out_specs=[VMEM] * 2,
        out_shape=[
            jax.ShapeDtypeStruct((share, RANK), F32),
            jax.ShapeDtypeStruct((RANK, share), F32),
        ],
        scratch_shapes=[
            pltpu.VMEM((groups, RANK, RANK), BF),
            pltpu.VMEM((groups, RANK, RANK), BF),
        ],
        compiler_params=PARAMS,
    )(scalars(sec % 4), *cols, factors)


def last_kernel(
    layers,
    place_ref, down_ref, up_ref, mixed_ref, slice_ref, out_ref,
    grad_down_ref, grad_up_ref,
    coef,
):
    sec = place_ref[0]
    groups = mixed_ref.shape[0]
    share = out_ref.shape[1]
    chunk = coef.shape[0] // groups
    for at in range(groups):
        coef[at * chunk:(at + 1) * chunk, :] = mixed_ref[at, :chunk, :]

    def block(index):
        return coef[index * RANK:(index + 1) * RANK, :]

    total_down = down_ref[...] + dot_tn(out_ref[...], block(0))
    total_up = up_ref[...] - dot_tn(block(layers + 1), out_ref[...])
    turned = jnp.zeros((share, RANK), F32)
    for l in range(layers):
        pair = block(l + 1)
        zero = jnp.zeros_like(pair)
        up = jnp.concatenate(
            [
                slice_ref[l, share + m * RANK:share + (m + 1) * RANK, :]
                for m in range(share // RANK)
            ],
            axis=1,
        )
        total_down += dot_tn(up, jnp.where(l < sec, pair, zero))
        turned += dot_nn(slice_ref[l, :share, :], jnp.where(l > sec, pair, zero))
        total_up -= dot_tn(block(layers + 2 + l), up)
    grad_down_ref[...] = total_down
    grad_up_ref[...] = total_up + turned.T


def last_products(sec, down, up, mixed, slices, out):
    layers = slices.shape[0]
    share = out.shape[1]
    return pl.pallas_call(
        functools.partial(last_kernel, layers),
        in_specs=[SMEM] + [VMEM] * 5,
        out_specs=[VMEM] * 2,
        out_shape=[
            jax.ShapeDtypeStruct((share, RANK), F32),
            jax.ShapeDtypeStruct((RANK, share), F32),
        ],
        scratch_shapes=[pltpu.VMEM(((2 * layers + 2) * RANK, RANK), BF)],
        compiler_params=PARAMS,
    )(scalars(sec), down, up, mixed, slices, out)


def spread(value, axis):
    count = lax.axis_size(axis)
    return lax.all_to_all(jnp.broadcast_to(value[None], (count,) + value.shape), axis, 0, 0)


def shards(text, cotangent, dec_down, dec_up, images, enc_down, enc_up, proj_in, proj_out, frame):
    sections = lax.axis_size("section")
    groups = lax.axis_size("dp")
    sec = lax.axis_index("section")
    grp = lax.axis_index("dp")
    core = sec % 2
    slot_count, patch_count, enc_width = images.shape[2:]
    tokens = patch_count // 4
    rows_total, width = text.shape[1:]
    rank = dec_down.shape[2]
    weight_down = dec_down[0]
    weight_up = dec_up[0]
    frames = frame[0]
    text = text[0]
    cot = cotangent[0]
    piece = rank // groups
    swap = [(at, at ^ 1) for at in range(sections)]

    up_rows = spread(lax.dynamic_slice_in_dim(weight_up, grp * piece, piece, 0), "section")

    slot_row = jnp.repeat(frames, tokens)[None, :]
    row = jnp.arange(rows_total, dtype=jnp.int32)[:, None]
    column = jnp.arange(rows_total, dtype=jnp.int32)[None, :]
    sel = (slot_row == row // tokens) & (row % tokens == column % tokens)
    keep = 1.0 - jnp.any(sel, axis=1, keepdims=True).astype(F32)
    sel = sel.astype(BF)
    cols, proj, cot_image, text_norm, image_gram, picks, blocks, own_slices, out_slice = (
        text_products(
            sec, grp, keep, text, cot, weight_down, weight_up, proj_out, sections, groups
        )
    )
    own_images = images[0, 0].reshape(slot_count * tokens, 4, enc_width).transpose(1, 0, 2)

    image_rows = lax.dynamic_slice_in_dim(proj_out, grp * piece, piece, 0)
    up_rows, cols, own_images, image_rows = lax.optimization_barrier(
        (up_rows, cols, own_images, image_rows)
    )
    cols = lax.all_to_all(cols, "dp", 0, 0)
    group_images = lax.all_gather(own_images, "section", axis=0)
    own_slices, group_images = lax.optimization_barrier((own_slices, group_images))
    slices = lax.all_gather(own_slices, "section", axis=0)
    rows = jnp.concatenate([image_rows[None], up_rows], axis=0).reshape(-1, width)
    gram = jnp.stack(
        [
            dot_nn(rows, weight_down).reshape(sections + 1, piece, rank),
            dot_nt(rows, weight_up).reshape(sections + 1, piece, rank),
        ],
        axis=1,
    ).astype(BF).reshape(-1, rank)
    packed = pack_gram(core, lax.all_gather(gram, "section", axis=0), groups)
    packed, cols, proj = lax.optimization_barrier((packed, cols, proj))
    own_gram = lax.all_to_all(packed, "dp", 0, 0)

    gath = lax.all_gather(proj, "section", axis=0)
    quarters = proj_in.reshape(4, enc_width, rank)
    state, wide, in_window = encoder_front(sec, group_images, enc_down, enc_up, quarters)
    own_gram, gath, state, wide, in_window, cols = lax.optimization_barrier(
        (own_gram, gath, state, wide, in_window, cols)
    )
    other_gram = lax.ppermute(own_gram, "section", swap)
    far = [(at, at ^ 2) for at in range(sections)]
    far_cols = lax.ppermute(cols, "section", far)

    coef, factor, image = rank_space(
        sec, core, own_gram, other_gram, gath, state, cot_image, text_norm, image_gram, sel, width
    )
    coef = lax.all_to_all(coef.reshape(groups, -1, rank), "dp", 0, 0)
    factor, slices = lax.optimization_barrier((factor, slices))
    factors = lax.all_gather(factor, "dp", axis=0)

    parts, (n_enc, n_in, pad_enc, pad_in) = encoder_late(
        sec, image, state, wide, in_window, blocks, enc_width, sections, groups
    )
    coef = jnp.sum(coef.astype(F32), axis=0).astype(BF)
    coef, far_cols = lax.optimization_barrier((coef, far_cols))
    chunk = coef.shape[0]
    mixed = jnp.concatenate(
        [jnp.broadcast_to(coef[None], (groups,) + coef.shape), parts], axis=1
    )
    mixed = lax.all_to_all(mixed, "dp", 0, 0)

    first_coef = mixed[0, :rank]
    at = (sections + 1) * rank
    last_coef = mixed[at // chunk, at % chunk:at % chunk + rank]
    few = picks.shape[2]
    term = dot_nt(picks[:, 0].reshape(-1, rank), first_coef)
    term = term - dot_nt(picks[:, 1].reshape(-1, rank), last_coef)
    term = lax.all_to_all(term.astype(BF).reshape(sections, few, rank), "section", 0, 0)

    every_cols = (
        cols, lax.ppermute(cols, "section", swap),
        far_cols, lax.ppermute(far_cols, "section", swap),
    )
    row_down, row_up = row_products(sec, every_cols, factors)
    grad_dec_down, grad_dec_up = last_products(
        sec, row_down, row_up, mixed, slices, out_slice
    )
    parts = jnp.sum(mixed[:, chunk:].astype(F32), axis=0)
    grad_enc_down = parts[:n_enc]
    grad_enc_up = parts[pad_enc:pad_enc + n_enc].T
    grad_proj_in = parts[2 * pad_enc:2 * pad_enc + n_in]
    own_out = parts[2 * pad_enc + pad_in:]
    grad_proj_out = (own_out + jnp.sum(term.astype(F32), axis=0)).T
    return (
        grad_dec_down[None],
        grad_dec_up[None],
        grad_enc_down,
        grad_enc_up,
        grad_proj_in,
        grad_proj_out,
    )


def solution(mesh):
    placed = (
        P("dp", None, None),
        P("dp", None, None),
        P("section", None, None),
        P("section", None, None),
        P("dp", "section", None, None, None),
        P(),
        P(),
        P(),
        P(),
        P("dp", None),
    )
    return jax.shard_map(
        shards,
        mesh=mesh,
        in_specs=placed,
        out_specs=(
            P("section", "dp", None),
            P("section", None, "dp"),
            P(("section", "dp"), None),
            P(None, ("section", "dp")),
            P(("section", "dp"), None),
            P(None, ("section", "dp")),
        ),
        check_vma=False,
    )
```

```python
import functools

import jax
import jax.numpy as jnp
from jax import lax
from jax.experimental import pallas as pl
from jax.experimental.pallas import tpu as pltpu
from jax.sharding import PartitionSpec as P

EPS = 1e-06
GELU_C = 0.7978845608028654
BF = jnp.bfloat16
F32 = jnp.float32


def gelu_tanh(value):
    return 0.5 * value * (1.0 + jnp.tanh(GELU_C * (value + 0.044715 * value * value * value)))


def gelu_slope(value):
    inner = jnp.tanh(GELU_C * (value + 0.044715 * value * value * value))
    return 0.5 * (1.0 + inner) + 0.5 * value * (1.0 - inner * inner) * GELU_C * (
        1.0 + 3.0 * 0.044715 * value * value
    )


def norm_scale(rows32):
    return lax.rsqrt(jnp.mean(rows32 * rows32, axis=-1, keepdims=True) + EPS)


def dot(left, right, dims):
    return lax.dot_general(left, right, ((dims[:1], dims[1:]), ((), ())), preferred_element_type=F32)


def dot_nn(left, right):
    return dot(left, right, (1, 0))


def dot_tn(left, right):
    return dot(left, right, (0, 0))


def dot_nt(left, right):
    return dot(left, right, (1, 1))


RANK = 128
VMEM = pl.BlockSpec(memory_space=pltpu.VMEM)
SMEM = pl.BlockSpec(memory_space=pltpu.SMEM)
PARAMS = pltpu.CompilerParams(vmem_limit_bytes=48 * 1024 * 1024)


def scalars(*values):
    return jnp.stack(values).astype(jnp.int32)


def text_kernel(
    part, share, few, steps,
    place_ref, keep_ref, text_ref, cot_ref, down_ref, up_ref, out_ref,
    cols_ref, proj_ref, base_ref,
    pick_ref, block_ref, slice_ref, out_slice_ref,
    proj, image, gram, norm,
):
    step = pl.program_id(0)
    sec, grp = place_ref[0], place_ref[1]

    @pl.when(step == 0)
    def _():
        proj[...] = jnp.zeros_like(proj)
        image[...] = jnp.zeros_like(image)
        gram[...] = jnp.zeros_like(gram)
        norm[...] = jnp.zeros_like(norm)

    text32 = text_ref[...].astype(F32) * keep_ref[...]
    text = text32.astype(BF)
    cot = cot_ref[...]
    norm[...] += jnp.sum(text32 * text32, axis=1, keepdims=True)
    proj[:RANK] += dot_nn(text, down_ref[...])
    proj[RANK:2 * RANK] += dot_nt(text, up_ref[...])
    proj[2 * RANK:] += dot_nt(cot, up_ref[...])
    image[...] += dot_nt(cot, out_ref[...])
    gram[...] += dot_nt(out_ref[...], out_ref[...])

    own = pl.ds(pl.multiple_of(lax.rem(sec, 4) * part, part), part)
    keep = keep_ref[own, :]
    pieces = cols_ref.shape[0]
    for piece in range(pieces):
        span = slice(piece * share, (piece + 1) * share)
        cols_ref[piece, :part, :] = (text_ref[own, span].astype(F32) * keep).astype(BF)
        cols_ref[piece, part:, :] = cot_ref[own, span]

    pick_ref[0, 0] = down_ref[pl.ds(pl.multiple_of(grp * few, few), few), :]
    per = RANK // few
    lanes = up_ref[:, pl.ds(pl.multiple_of(grp // per * RANK, RANK), RANK)].astype(F32).T
    picked = lanes[:few]
    for at in range(1, per):
        picked = jnp.where(lax.rem(grp, per) == at, lanes[at * few:(at + 1) * few], picked)
    pick_ref[0, 1] = picked.astype(BF)

    @pl.when(step == sec)
    def _():
        block_ref[0] = cot
        block_ref[1] = out_ref[...]

    @pl.when(step == grp // pieces)
    def _():
        at = pl.multiple_of(lax.rem(grp, pieces) * share, share)
        slice_ref[:share, :] = down_ref[pl.ds(at, share), :]
        up = up_ref[:, pl.ds(at, share)]
        for m in range(share // RANK):
            slice_ref[share + m * RANK:share + (m + 1) * RANK, :] = up[:, m * RANK:(m + 1) * RANK]
        out_slice_ref[...] = out_ref[:, pl.ds(at, share)]

    @pl.when(step == steps - 1)
    def _():
        proj_ref[:3 * RANK, :] = proj[...].astype(BF)
        proj_ref[3 * RANK:, :] = jnp.zeros((RANK, RANK), BF)
        base_ref[0] = image[...]
        base_ref[1] = gram[...]
        base_ref[2] = jnp.broadcast_to(norm[...], (RANK, RANK))


def text_products(sec, grp, keep, text, cot, down, up, out, sections, groups):
    rows, width = text.shape
    share = width // groups
    steps = sections
    wide = width // steps
    pieces = wide // share
    few = wide // groups
    part = rows // 4
    across = pl.BlockSpec((rows, wide), lambda i: (0, i))
    column = pl.BlockSpec((rows, 1), lambda i: (0, 0))
    return pl.pallas_call(
        functools.partial(text_kernel, part, share, few, steps),
        grid=(steps,),
        in_specs=[
            SMEM,
            column,
            across,
            across,
            pl.BlockSpec((wide, RANK), lambda i: (i, 0)),
            across,
            across,
        ],
        out_specs=[
            pl.BlockSpec((pieces, 2 * part, share), lambda i: (i, 0, 0)),
            pl.BlockSpec((4 * RANK, RANK), lambda i: (0, 0)),
            pl.BlockSpec((3, RANK, RANK), lambda i: (0, 0, 0)),
            pl.BlockSpec((1, 2, few, RANK), lambda i: (i, 0, 0, 0)),
            pl.BlockSpec((2, rows, wide), lambda i: (0, 0, 0)),
            pl.BlockSpec((2 * share, RANK), lambda i: (0, 0)),
            pl.BlockSpec((rows, share), lambda i: (0, 0)),
        ],
        out_shape=[
            jax.ShapeDtypeStruct((groups, 2 * part, share), BF),
            jax.ShapeDtypeStruct((4 * RANK, RANK), BF),
            jax.ShapeDtypeStruct((3, RANK, RANK), F32),
            jax.ShapeDtypeStruct((steps, 2, few, RANK), BF),
            jax.ShapeDtypeStruct((2, rows, wide), BF),
            jax.ShapeDtypeStruct((2 * share, RANK), BF),
            jax.ShapeDtypeStruct((rows, share), BF),
        ],
        scratch_shapes=[
            pltpu.VMEM((3 * RANK, RANK), F32),
            pltpu.VMEM((rows, RANK), F32),
            pltpu.VMEM((RANK, RANK), F32),
            pltpu.VMEM((rows, 1), F32),
        ],
        compiler_params=PARAMS,
    )(scalars(sec, grp), keep, text, cot, down, up, out)


def window(width, count):
    block = width // count
    stride = block // RANK * RANK
    tiles = -(-((count - 1) * (block - stride) + block) // RANK)
    return stride, tiles


def front_kernel(
    sections, windows, in_windows,
    place_ref, image_ref, down_ref, up_ref, in_ref,
    state_ref, pre_ref, wide_ref, in_window_ref,
    normed_buf, out_buf,
):
    sec = place_ref[0]
    width = down_ref.shape[0]
    span = windows[1] * RANK
    own = pl.ds(pl.multiple_of(sec * windows[0], RANK), span)
    total = jnp.zeros((RANK, 1), F32)
    for k in range(4):
        patch = jnp.concatenate([image_ref[l, k] for l in range(sections)], axis=0).astype(F32)
        normed = (patch * norm_scale(patch)).astype(BF)
        normed_buf[...] = normed
        pre = dot_nn(normed, down_ref[...])
        act = gelu_tanh(pre).astype(BF)
        out = (patch + dot_nn(act, up_ref[...])).astype(BF)
        out_buf[k] = out
        out32 = out.astype(F32)
        total = total + jnp.sum(out32 * out32, axis=1, keepdims=True)
        state_ref[k] = gelu_slope(pre)
        state_ref[4 + k] = dot_nt(out, up_ref[...])
        wide_ref[:, k * RANK:(k + 1) * RANK] = act
        cross = dot(in_ref[k], up_ref[...], (0, 1))
        wide_ref[:, (4 + k) * RANK:(5 + k) * RANK] = cross.astype(BF)
        at = 8 * RANK + k * span
        wide_ref[:, at:at + span] = normed_buf[:, own]
        at += 4 * span
        wide_ref[:, at:at + span] = out_buf[k, :, own]
        in_window_ref[k * span:(k + 1) * span, :] = in_ref[k, own, :]
    scale = lax.rsqrt(total * (1.0 / (4 * width)) + EPS)
    proj = jnp.zeros((RANK, RANK), F32)
    for k in range(4):
        proj = proj + dot_nn((out_buf[k].astype(F32) * scale).astype(BF), in_ref[k])
    state_ref[8] = proj
    pre_ref[...] = proj
    state_ref[9] = jnp.broadcast_to(scale, (RANK, RANK))
    per = sections // 4
    own = pl.ds(
        pl.multiple_of(lax.rem(sec, per) * in_windows[0], RANK), in_windows[1] * RANK
    )
    out = out_buf[sec // per, :, own].astype(F32)
    wide_ref[:, 8 * RANK + 8 * span:] = (out * scale).astype(BF)


def encoder_front(sec, images, enc_down, enc_up, proj_in):
    sections = images.shape[0]
    width = images.shape[3]
    windows = window(width, sections)
    in_windows = window(width, sections // 4)
    span = windows[1] * RANK
    total = 8 * RANK + 8 * span + in_windows[1] * RANK
    return pl.pallas_call(
        functools.partial(front_kernel, sections, windows, in_windows),
        in_specs=[SMEM] + [VMEM] * 4,
        out_specs=[VMEM] * 4,
        out_shape=[
            jax.ShapeDtypeStruct((10, RANK, RANK), F32),
            jax.ShapeDtypeStruct((RANK, RANK), F32),
            jax.ShapeDtypeStruct((RANK, total), BF),
            jax.ShapeDtypeStruct((4 * span, RANK), BF),
        ],
        scratch_shapes=[
            pltpu.VMEM((RANK, width), BF),
            pltpu.VMEM((4, RANK, width), BF),
        ],
        compiler_params=PARAMS,
    )(scalars(sec), images, enc_down, enc_up, proj_in)


def two_lanes(column):
    high = column.astype(BF).astype(F32)
    lane = lax.broadcasted_iota(jnp.int32, (column.shape[0], RANK), 1)
    zero = jnp.zeros((column.shape[0], RANK), F32)
    return jnp.where(lane == 0, high, jnp.where(lane == 1, column - high, zero))


def pack_kernel(layers, core_ref, gram_ref, out_ref, packed):
    at = 0
    for l in range(layers):
        size = (l + 2) * 16
        packed[at:at + size, :] = gram_ref[l, :size, :]
        at += size
    half = at // 2
    value = packed[pl.ds(pl.multiple_of(core_ref[0] * half, 16), half), :]
    for to in range(out_ref.shape[0]):
        out_ref[to] = value


def pack_gram(core, gram, groups):
    layers = gram.shape[0]
    total = sum((l + 2) * 16 for l in range(layers))
    return pl.pallas_call(
        functools.partial(pack_kernel, layers),
        in_specs=[SMEM, VMEM],
        out_specs=VMEM,
        out_shape=jax.ShapeDtypeStruct((groups, total // 2, RANK), BF),
        scratch_shapes=[pltpu.VMEM((total, RANK), BF)],
        compiler_params=PARAMS,
    )(scalars(core), gram)


def rank_kernel(
    layers, width,
    place_ref, own_ref, other_ref, gath_ref, proj_pre_ref, base_ref, sel_ref,
    coef_ref, factor_ref, image_ref,
    weight, acts, act_cat, grads, scaled, back, pre_ref, slope_ref, inner_ref, scale_ref, sums_ref,
):
    rank = RANK
    own = place_ref[0]
    core = place_ref[1]
    at = 0
    for l in range(layers):
        for j in range(l + 2):
            which, place = divmod(at, own_ref.shape[1])
            span = slice(place, place + 16)
            tile = jnp.where(core == which, own_ref[:, span, :], other_ref[:, span, :])
            tile = tile.astype(F32)
            rows = slice(j * rank, (j + 1) * rank)
            weight[l, rows, :rank] = tile[:, :8, :].reshape(rank, rank).astype(BF)
            weight[l, rows, rank:] = tile[:, 8:, :].reshape(rank, rank).astype(BF)
            at += 16

    proj_pre = proj_pre_ref[...]
    sel = sel_ref[...]
    placed = dot_nn(sel, gelu_tanh(proj_pre).astype(BF))
    placed_half = placed.astype(BF)
    acts[0] = placed_half
    act_cat[:, :rank] = placed_half
    image_inner = dot_nn(placed_half, base_ref[1].astype(BF))
    total = base_ref[2][:, :1] + jnp.sum(placed * image_inner, axis=1, keepdims=True)
    for l in range(layers):
        here = (l + 1) * rank
        scale = lax.rsqrt(jnp.maximum(total, 0.0) * (1.0 / width) + EPS)
        both = dot_nn(act_cat[:, :here], weight[l, :here, :])
        pre = scale * (gath_ref[l, :rank, :].astype(F32) + both[:, :rank])
        inner = gath_ref[l, rank:2 * rank, :].astype(F32) + both[:, rank:]
        sig = jax.nn.sigmoid(pre)
        act = (pre * sig).astype(BF)
        acts[l + 1] = act
        act_cat[:, here:here + rank] = act
        after = inner + dot_nn(act, weight[l, here:here + rank, rank:])
        total = total + jnp.sum(act.astype(F32) * (inner + after), axis=1, keepdims=True)
        pre_ref[l] = pre
        slope_ref[l] = sig * (1.0 + pre * (1.0 - sig))
        inner_ref[l] = after
        scale_ref[l] = scale
    back[...] = jnp.zeros_like(back)
    sums = jnp.zeros_like(total)
    for l in reversed(range(layers)):
        here = (l + 1) * rank
        cot = gath_ref[l, 2 * rank:3 * rank, :].astype(F32)
        d_act = cot - sums * inner_ref[l] + back[:, here:here + rank]
        d_pre = (d_act * slope_ref[l]).astype(BF).astype(F32)
        scale = scale_ref[l]
        mean = jnp.sum(d_pre * pre_ref[l], axis=1, keepdims=True) * (1.0 / width)
        grad = (scale * d_pre).astype(BF)
        part = (sums * acts[l + 1].astype(F32)).astype(BF)
        grads[l] = grad
        scaled[l + 1] = part
        sums_ref[l] = sums
        pair = jnp.concatenate([grad, -part], axis=1)
        back[:, :here] += dot_nt(pair, weight[l, :here, :])
        sums = sums + scale * scale * mean
    d_image = base_ref[0] - sums * image_inner + back[:, :rank]
    scaled[0] = (sums * placed).astype(BF)
    d_slot = dot_tn(sel, d_image.astype(BF))
    image_ref[0] = (d_slot * gelu_slope(proj_pre)).astype(BF)
    image_ref[1] = placed_half
    image_ref[2] = scaled[0]

    own_act = acts[own + 1]
    own_grad = grads[own]
    own_scaled = scaled[own + 1]
    factor_ref[:rank, :] = own_grad
    factor_ref[rank:2 * rank, :] = own_act
    factor_ref[2 * rank:, :] = two_lanes(sums_ref[own]).T[:16].astype(BF)
    coef_ref[0] = dot_tn(acts[0], own_grad).astype(BF)
    for l in range(layers):
        low = l < own
        left = jnp.where(low, acts[l + 1], grads[l])
        right = jnp.where(low, own_grad, own_act)
        coef_ref[l + 1] = dot_tn(left, right).astype(BF)
    for l in range(layers + 1):
        low = l <= own + 1
        left = jnp.where(low, acts[l], scaled[l])
        right = jnp.where(low, own_scaled, own_act)
        coef_ref[layers + 1 + l] = dot_tn(left, right).astype(BF)


def rank_space(position, core, gram, other, gath, proj_pre, base, sel, width):
    layers = gath.shape[0]
    rank = RANK
    tall = (layers + 1) * rank
    operands = (gram, other, gath, proj_pre, base, sel)

    def whole(shape):
        return pl.BlockSpec(shape, lambda i: (0,) * len(shape))

    outs = ((2 * layers + 2, rank, rank), (2 * rank + 16, rank), (3, rank, rank))
    return pl.pallas_call(
        functools.partial(rank_kernel, layers, width),
        grid=(1,),
        in_specs=[SMEM] + [whole(value.shape) for value in operands],
        out_specs=[whole(shape) for shape in outs],
        out_shape=[jax.ShapeDtypeStruct(shape, BF) for shape in outs],
        scratch_shapes=[
            pltpu.VMEM((layers, tall, 2 * rank), BF),
            pltpu.VMEM((layers + 1, rank, rank), BF),
            pltpu.VMEM((rank, tall), BF),
            pltpu.VMEM((layers, rank, rank), BF),
            pltpu.VMEM((layers + 1, rank, rank), BF),
            pltpu.VMEM((rank, tall), F32),
            pltpu.VMEM((layers, rank, rank), F32),
            pltpu.VMEM((layers, rank, rank), F32),
            pltpu.VMEM((layers, rank, rank), F32),
            pltpu.VMEM((layers, rank, 1), F32),
            pltpu.VMEM((layers, rank, 1), F32),
        ],
        compiler_params=pltpu.CompilerParams(vmem_limit_bytes=60 * 1024 * 1024),
    )(scalars(position, core), *operands)


def late_kernel(
    enc_width, tiles, in_tiles, pieces,
    shift_ref, image_ref, state_ref, wide_ref, in_ref, block_ref,
    part_ref,
    down, up, proj, last,
):
    span = tiles * RANK
    d_proj = image_ref[0]
    placed = image_ref[1]
    d_proj32 = d_proj.astype(F32)
    proj_scale = state_ref[9]
    mean = jnp.sum(d_proj32 * state_ref[8], axis=1, keepdims=True) * (1.0 / (4 * enc_width))
    d_scaled = (d_proj32 * proj_scale).astype(BF)
    pull = mean * proj_scale * proj_scale
    total_down = jnp.zeros((span, RANK), F32)
    total_up = jnp.zeros((span, RANK), F32)
    for k in range(4):
        act = wide_ref[:, k * RANK:(k + 1) * RANK]
        cross = wide_ref[:, (4 + k) * RANK:(5 + k) * RANK]
        at = 8 * RANK + k * span
        normed = wide_ref[:, at:at + span]
        at += 4 * span
        out = wide_ref[:, at:at + span]
        d_enc = (dot_nn(d_scaled, cross) - pull * state_ref[4 + k]) * state_ref[k]
        total_down += dot_tn(normed, d_enc.astype(BF))
        inner = dot_tn(d_scaled, act).astype(BF)
        total_up += dot_nn(in_ref[k * span:(k + 1) * span, :], inner)
        total_up -= dot_tn(out, (pull * act.astype(F32)).astype(BF))
    down[:span, :] = total_down
    up[:span, :] = total_up
    proj[:in_tiles * RANK, :] = dot_tn(wide_ref[:, 8 * RANK + 8 * span:], d_proj)
    last[...] = dot_tn(block_ref[0], placed) - dot_tn(
        block_ref[1], dot_tn(placed, image_ref[2]).astype(BF)
    )
    groups = part_ref.shape[0]
    n_enc, n_in, pad_enc, pad_in = pieces
    n_out = last.shape[0] // groups
    for to in range(groups):
        at = shift_ref[0] + n_enc * to
        part_ref[to, :pad_enc, :] = down[pl.ds(at, pad_enc), :].astype(BF)
        part_ref[to, pad_enc:2 * pad_enc, :] = up[pl.ds(at, pad_enc), :].astype(BF)
        at = shift_ref[1] + n_in * to
        part_ref[to, 2 * pad_enc:2 * pad_enc + pad_in, :] = proj[pl.ds(at, pad_in), :].astype(BF)
        part_ref[to, 2 * pad_enc + pad_in:, :] = last[to * n_out:(to + 1) * n_out, :].astype(BF)


def encoder_late(sec, image, state, wide, in_window, blocks, enc_width, sections, groups):
    tiles = window(enc_width, sections)[1]
    in_tiles = window(enc_width, sections // 4)[1]
    block = enc_width // sections
    in_block = 4 * block
    n_enc = block // groups
    n_in = in_block // groups
    pad_enc = -(-n_enc // 16) * 16
    pad_in = -(-n_in // 16) * 16
    shifts = scalars(
        sec * (block % RANK), (sec % (sections // 4)) * (in_block % RANK)
    )
    columns = blocks.shape[2]
    total = 2 * pad_enc + pad_in + columns // groups
    pieces = (n_enc, n_in, pad_enc, pad_in)
    parts = pl.pallas_call(
        functools.partial(late_kernel, enc_width, tiles, in_tiles, pieces),
        in_specs=[SMEM] + [VMEM] * 5,
        out_specs=VMEM,
        out_shape=jax.ShapeDtypeStruct((groups, total, RANK), BF),
        scratch_shapes=[
            pltpu.VMEM((tiles * RANK + 16, RANK), F32),
            pltpu.VMEM((tiles * RANK + 16, RANK), F32),
            pltpu.VMEM((in_tiles * RANK + 16, RANK), F32),
            pltpu.VMEM((columns, RANK), F32),
        ],
        compiler_params=PARAMS,
    )(shifts, image, state, wide, in_window, blocks)
    return parts, pieces


def row_kernel(
    place_ref, first_ref, second_ref, third_ref, fourth_ref, factor_ref,
    down_ref, up_ref,
    acts, scaled,
):
    groups, rows, share = first_ref.shape
    part = rows // 2
    for at in range(groups):
        act = factor_ref[at, RANK:2 * RANK, :]
        weights = factor_ref[at, 2 * RANK:2 * RANK + 8, :].astype(F32)
        weights = jnp.sum(weights, axis=0, keepdims=True)
        weights = jnp.broadcast_to(weights, (RANK, RANK)).T
        acts[at] = act
        scaled[at] = (act.astype(F32) * weights).astype(BF)

    def flat(value):
        return value.reshape(groups * part, value.shape[-1])

    total_down = jnp.zeros((share, RANK), F32)
    total_up = jnp.zeros((RANK, share), F32)
    own = place_ref[0]
    for at, cols_ref in enumerate((first_ref, second_ref, third_ref, fourth_ref)):
        which = lax.rem(own, 2) if at % 2 == 0 else 1 - lax.rem(own, 2)
        which = which + 2 * (own // 2 if at < 2 else 1 - own // 2)
        start = pl.multiple_of(which * part, part)
        text = flat(cols_ref[:, :part, :])
        cot = flat(cols_ref[:, part:, :])
        total_down += dot_tn(text, flat(factor_ref[:, pl.ds(start, part), :]))
        total_up += dot_tn(flat(acts[:, pl.ds(start, part), :]), cot)
        total_up -= dot_tn(flat(scaled[:, pl.ds(start, part), :]), text)
    down_ref[...] = total_down
    up_ref[...] = total_up


def row_products(sec, cols, factors):
    groups, _, share = cols[0].shape
    return pl.pallas_call(
        row_kernel,
        in_specs=[SMEM] + [VMEM] * 5,
        out_specs=[VMEM] * 2,
        out_shape=[
            jax.ShapeDtypeStruct((share, RANK), F32),
            jax.ShapeDtypeStruct((RANK, share), F32),
        ],
        scratch_shapes=[
            pltpu.VMEM((groups, RANK, RANK), BF),
            pltpu.VMEM((groups, RANK, RANK), BF),
        ],
        compiler_params=PARAMS,
    )(scalars(sec % 4), *cols, factors)


def last_kernel(
    layers,
    place_ref, down_ref, up_ref, mixed_ref, slice_ref, out_ref,
    grad_down_ref, grad_up_ref,
    coef,
):
    sec = place_ref[0]
    groups = mixed_ref.shape[0]
    share = out_ref.shape[1]
    chunk = coef.shape[0] // groups
    for at in range(groups):
        coef[at * chunk:(at + 1) * chunk, :] = mixed_ref[at, :chunk, :]

    def block(index):
        return coef[index * RANK:(index + 1) * RANK, :]

    total_down = down_ref[...] + dot_tn(out_ref[...], block(0))
    total_up = up_ref[...] - dot_tn(block(layers + 1), out_ref[...])
    turned = jnp.zeros((share, RANK), F32)
    for l in range(layers):
        pair = block(l + 1)
        zero = jnp.zeros_like(pair)
        up = jnp.concatenate(
            [
                slice_ref[l, share + m * RANK:share + (m + 1) * RANK, :]
                for m in range(share // RANK)
            ],
            axis=1,
        )
        total_down += dot_tn(up, jnp.where(l < sec, pair, zero))
        turned += dot_nn(slice_ref[l, :share, :], jnp.where(l > sec, pair, zero))
        total_up -= dot_tn(block(layers + 2 + l), up)
    grad_down_ref[...] = total_down
    grad_up_ref[...] = total_up + turned.T


def last_products(sec, down, up, mixed, slices, out):
    layers = slices.shape[0]
    share = out.shape[1]
    return pl.pallas_call(
        functools.partial(last_kernel, layers),
        in_specs=[SMEM] + [VMEM] * 5,
        out_specs=[VMEM] * 2,
        out_shape=[
            jax.ShapeDtypeStruct((share, RANK), F32),
            jax.ShapeDtypeStruct((RANK, share), F32),
        ],
        scratch_shapes=[pltpu.VMEM(((2 * layers + 2) * RANK, RANK), BF)],
        compiler_params=PARAMS,
    )(scalars(sec), down, up, mixed, slices, out)


def spread(value, axis):
    count = lax.axis_size(axis)
    return lax.all_to_all(jnp.broadcast_to(value[None], (count,) + value.shape), axis, 0, 0)


def shards(text, cotangent, dec_down, dec_up, images, enc_down, enc_up, proj_in, proj_out, frame):
    sections = lax.axis_size("section")
    groups = lax.axis_size("dp")
    sec = lax.axis_index("section")
    grp = lax.axis_index("dp")
    core = sec % 2
    slot_count, patch_count, enc_width = images.shape[2:]
    tokens = patch_count // 4
    rows_total, width = text.shape[1:]
    rank = dec_down.shape[2]
    weight_down = dec_down[0]
    weight_up = dec_up[0]
    frames = frame[0]
    text = text[0]
    cot = cotangent[0]
    piece = rank // groups
    swap = [(at, at ^ 1) for at in range(sections)]

    own_rows = lax.dynamic_slice_in_dim(weight_up, grp * piece, piece, 0)
    own_rows, frames = lax.optimization_barrier((own_rows, frames))
    up_rows = spread(own_rows, "section")

    slot_row = jnp.repeat(frames, tokens)[None, :]
    row = jnp.arange(rows_total, dtype=jnp.int32)[:, None]
    column = jnp.arange(rows_total, dtype=jnp.int32)[None, :]
    sel = (slot_row == row // tokens) & (row % tokens == column % tokens)
    keep = 1.0 - jnp.any(sel, axis=1, keepdims=True).astype(F32)
    sel = sel.astype(BF)
    cols, proj, base, picks, blocks, own_slices, out_slice = (
        text_products(
            sec, grp, keep, text, cot, weight_down, weight_up, proj_out, sections, groups
        )
    )
    gath = lax.all_gather(proj, "section", axis=0)
    own_images = images[0, 0].reshape(slot_count * tokens, 4, enc_width).transpose(1, 0, 2)

    image_rows = lax.dynamic_slice_in_dim(proj_out, grp * piece, piece, 0)
    up_rows, cols, image_rows = lax.optimization_barrier((up_rows, cols, image_rows))
    cols = lax.all_to_all(cols, "dp", 0, 0)
    gath, own_images = lax.optimization_barrier((gath, own_images))
    group_images = lax.all_gather(own_images, "section", axis=0)
    own_slices, group_images = lax.optimization_barrier((own_slices, group_images))
    slices = lax.all_gather(own_slices, "section", axis=0)
    rows = jnp.concatenate([image_rows[None], up_rows], axis=0).reshape(-1, width)
    gram = jnp.stack(
        [
            dot_nn(rows, weight_down).reshape(sections + 1, piece, rank),
            dot_nt(rows, weight_up).reshape(sections + 1, piece, rank),
        ],
        axis=1,
    ).astype(BF).reshape(-1, rank)
    packed = pack_gram(core, lax.all_gather(gram, "section", axis=0), groups)
    packed, cols = lax.optimization_barrier((packed, cols))
    own_gram = lax.all_to_all(packed, "dp", 0, 0)

    quarters = proj_in.reshape(4, enc_width, rank)
    state, proj_pre, wide, in_window = encoder_front(
        sec, group_images, enc_down, enc_up, quarters
    )
    own_gram, gath, state, proj_pre, wide, in_window, cols = lax.optimization_barrier(
        (own_gram, gath, state, proj_pre, wide, in_window, cols)
    )
    other_gram = lax.ppermute(own_gram, "section", swap)
    far = [(at, at ^ 2) for at in range(sections)]
    far_cols = lax.ppermute(cols, "section", far)

    gath, slices = lax.optimization_barrier((gath, slices))
    coef, factor, image = rank_space(
        sec, core, own_gram, other_gram, gath, proj_pre, base, sel, width
    )
    coef = lax.all_to_all(coef.reshape(groups, -1, rank), "dp", 0, 0)
    factors = lax.all_gather(factor, "dp", axis=0)

    parts, (n_enc, n_in, pad_enc, pad_in) = encoder_late(
        sec, image, state, wide, in_window, blocks, enc_width, sections, groups
    )
    coef = jnp.sum(coef.astype(F32), axis=0).astype(BF)
    coef, far_cols = lax.optimization_barrier((coef, far_cols))
    chunk = coef.shape[0]
    mixed = jnp.concatenate(
        [jnp.broadcast_to(coef[None], (groups,) + coef.shape), parts], axis=1
    )
    mixed = lax.all_to_all(mixed, "dp", 0, 0)

    first_coef = mixed[0, :rank]
    at = (sections + 1) * rank
    last_coef = mixed[at // chunk, at % chunk:at % chunk + rank]
    few = picks.shape[2]
    term = dot_nt(picks[:, 0].reshape(-1, rank), first_coef)
    term = term - dot_nt(picks[:, 1].reshape(-1, rank), last_coef)
    term = lax.all_to_all(term.astype(BF).reshape(sections, few, rank), "section", 0, 0)

    every_cols = (
        cols, lax.ppermute(cols, "section", swap),
        far_cols, lax.ppermute(far_cols, "section", swap),
    )
    row_down, row_up = row_products(sec, every_cols, factors)
    grad_dec_down, grad_dec_up = last_products(
        sec, row_down, row_up, mixed, slices, out_slice
    )
    parts = jnp.sum(mixed[:, chunk:].astype(F32), axis=0)
    grad_enc_down = parts[:n_enc]
    grad_enc_up = parts[pad_enc:pad_enc + n_enc].T
    grad_proj_in = parts[2 * pad_enc:2 * pad_enc + n_in]
    own_out = parts[2 * pad_enc + pad_in:]
    grad_proj_out = (own_out + jnp.sum(term.astype(F32), axis=0)).T
    return (
        grad_dec_down[None],
        grad_dec_up[None],
        grad_enc_down,
        grad_enc_up,
        grad_proj_in,
        grad_proj_out,
    )


def solution(mesh):
    placed = (
        P("dp", None, None),
        P("dp", None, None),
        P("section", None, None),
        P("section", None, None),
        P("dp", "section", None, None, None),
        P(),
        P(),
        P(),
        P(),
        P("dp", None),
    )
    return jax.shard_map(
        shards,
        mesh=mesh,
        in_specs=placed,
        out_specs=(
            P("section", "dp", None),
            P("section", None, "dp"),
            P(("section", "dp"), None),
            P(None, ("section", "dp")),
            P(("section", "dp"), None),
            P(None, ("section", "dp")),
        ),
        check_vma=False,
    )
```

```python
import functools

import jax
import jax.numpy as jnp
from jax import lax
from jax.experimental import pallas as pl
from jax.experimental.pallas import tpu as pltpu
from jax.sharding import PartitionSpec as P

EPS = 1e-06
GELU_C = 0.7978845608028654
BF = jnp.bfloat16
F32 = jnp.float32


def gelu_tanh(value):
    return 0.5 * value * (1.0 + jnp.tanh(GELU_C * (value + 0.044715 * value * value * value)))


def gelu_slope(value):
    inner = jnp.tanh(GELU_C * (value + 0.044715 * value * value * value))
    return 0.5 * (1.0 + inner) + 0.5 * value * (1.0 - inner * inner) * GELU_C * (
        1.0 + 3.0 * 0.044715 * value * value
    )


def norm_scale(rows32):
    return lax.rsqrt(jnp.mean(rows32 * rows32, axis=-1, keepdims=True) + EPS)


def dot(left, right, dims):
    return lax.dot_general(left, right, ((dims[:1], dims[1:]), ((), ())), preferred_element_type=F32)


def dot_nn(left, right):
    return dot(left, right, (1, 0))


def dot_tn(left, right):
    return dot(left, right, (0, 0))


def dot_nt(left, right):
    return dot(left, right, (1, 1))


RANK = 128
VMEM = pl.BlockSpec(memory_space=pltpu.VMEM)
SMEM = pl.BlockSpec(memory_space=pltpu.SMEM)
PARAMS = pltpu.CompilerParams(vmem_limit_bytes=48 * 1024 * 1024)


def scalars(*values):
    return jnp.stack(values).astype(jnp.int32)


def text_kernel(
    part, share, few, steps,
    place_ref, keep_ref, text_ref, cot_ref, down_ref, up_ref, out_ref,
    cols_ref, proj_ref, base_ref,
    pick_ref, block_ref, slice_ref, out_slice_ref,
    proj, image, gram, norm,
):
    step = pl.program_id(0)
    sec, grp = place_ref[0], place_ref[1]

    @pl.when(step == 0)
    def _():
        proj[...] = jnp.zeros_like(proj)
        image[...] = jnp.zeros_like(image)
        gram[...] = jnp.zeros_like(gram)
        norm[...] = jnp.zeros_like(norm)

    text32 = text_ref[...].astype(F32) * keep_ref[...]
    text = text32.astype(BF)
    cot = cot_ref[...]
    norm[...] += jnp.sum(text32 * text32, axis=1, keepdims=True)
    proj[:RANK] += dot_nn(text, down_ref[...])
    proj[RANK:2 * RANK] += dot_nt(text, up_ref[...])
    proj[2 * RANK:] += dot_nt(cot, up_ref[...])
    image[...] += dot_nt(cot, out_ref[...])
    gram[...] += dot_nt(out_ref[...], out_ref[...])

    own = pl.ds(pl.multiple_of(lax.rem(sec, 4) * part, part), part)
    keep = keep_ref[own, :]
    pieces = cols_ref.shape[0]
    for piece in range(pieces):
        span = slice(piece * share, (piece + 1) * share)
        cols_ref[piece, :part, :] = (text_ref[own, span].astype(F32) * keep).astype(BF)
        cols_ref[piece, part:, :] = cot_ref[own, span]

    pick_ref[0, 0] = down_ref[pl.ds(pl.multiple_of(grp * few, few), few), :]
    per = RANK // few
    lanes = up_ref[:, pl.ds(pl.multiple_of(grp // per * RANK, RANK), RANK)].astype(F32).T
    picked = lanes[:few]
    for at in range(1, per):
        picked = jnp.where(lax.rem(grp, per) == at, lanes[at * few:(at + 1) * few], picked)
    pick_ref[0, 1] = picked.astype(BF)

    @pl.when(step == sec)
    def _():
        block_ref[0] = cot
        block_ref[1] = out_ref[...]

    @pl.when(step == grp // pieces)
    def _():
        at = pl.multiple_of(lax.rem(grp, pieces) * share, share)
        slice_ref[:share, :] = down_ref[pl.ds(at, share), :]
        up = up_ref[:, pl.ds(at, share)]
        for m in range(share // RANK):
            slice_ref[share + m * RANK:share + (m + 1) * RANK, :] = up[:, m * RANK:(m + 1) * RANK]
        out_slice_ref[...] = out_ref[:, pl.ds(at, share)]

    @pl.when(step == steps - 1)
    def _():
        proj_ref[:3 * RANK, :] = proj[...].astype(BF)
        proj_ref[3 * RANK:, :] = jnp.zeros((RANK, RANK), BF)
        base_ref[0] = image[...]
        base_ref[1] = gram[...]
        base_ref[2] = jnp.broadcast_to(norm[...], (RANK, RANK))


def text_products(sec, grp, keep, text, cot, down, up, out, sections, groups):
    rows, width = text.shape
    share = width // groups
    steps = sections
    wide = width // steps
    pieces = wide // share
    few = wide // groups
    part = rows // 4
    across = pl.BlockSpec((rows, wide), lambda i: (0, i))
    column = pl.BlockSpec((rows, 1), lambda i: (0, 0))
    return pl.pallas_call(
        functools.partial(text_kernel, part, share, few, steps),
        grid=(steps,),
        in_specs=[
            SMEM,
            column,
            across,
            across,
            pl.BlockSpec((wide, RANK), lambda i: (i, 0)),
            across,
            across,
        ],
        out_specs=[
            pl.BlockSpec((pieces, 2 * part, share), lambda i: (i, 0, 0)),
            pl.BlockSpec((4 * RANK, RANK), lambda i: (0, 0)),
            pl.BlockSpec((3, RANK, RANK), lambda i: (0, 0, 0)),
            pl.BlockSpec((1, 2, few, RANK), lambda i: (i, 0, 0, 0)),
            pl.BlockSpec((2, rows, wide), lambda i: (0, 0, 0)),
            pl.BlockSpec((2 * share, RANK), lambda i: (0, 0)),
            pl.BlockSpec((rows, share), lambda i: (0, 0)),
        ],
        out_shape=[
            jax.ShapeDtypeStruct((groups, 2 * part, share), BF),
            jax.ShapeDtypeStruct((4 * RANK, RANK), BF),
            jax.ShapeDtypeStruct((3, RANK, RANK), F32),
            jax.ShapeDtypeStruct((steps, 2, few, RANK), BF),
            jax.ShapeDtypeStruct((2, rows, wide), BF),
            jax.ShapeDtypeStruct((2 * share, RANK), BF),
            jax.ShapeDtypeStruct((rows, share), BF),
        ],
        scratch_shapes=[
            pltpu.VMEM((3 * RANK, RANK), F32),
            pltpu.VMEM((rows, RANK), F32),
            pltpu.VMEM((RANK, RANK), F32),
            pltpu.VMEM((rows, 1), F32),
        ],
        compiler_params=PARAMS,
    )(scalars(sec, grp), keep, text, cot, down, up, out)


def window(width, count):
    block = width // count
    stride = block // RANK * RANK
    tiles = -(-((count - 1) * (block - stride) + block) // RANK)
    return stride, tiles


def front_kernel(
    sections, windows, in_windows,
    place_ref, image_ref, down_ref, up_ref, in_ref,
    state_ref, pre_ref, wide_ref, in_window_ref,
    normed_buf, out_buf,
):
    sec = place_ref[0]
    width = down_ref.shape[0]
    span = windows[1] * RANK
    own = pl.ds(pl.multiple_of(sec * windows[0], RANK), span)
    total = jnp.zeros((RANK, 1), F32)
    for k in range(4):
        patch = jnp.concatenate([image_ref[l, k] for l in range(sections)], axis=0).astype(F32)
        normed = (patch * norm_scale(patch)).astype(BF)
        normed_buf[...] = normed
        pre = dot_nn(normed, down_ref[...])
        act = gelu_tanh(pre).astype(BF)
        out = (patch + dot_nn(act, up_ref[...])).astype(BF)
        out_buf[k] = out
        out32 = out.astype(F32)
        total = total + jnp.sum(out32 * out32, axis=1, keepdims=True)
        state_ref[k] = gelu_slope(pre)
        state_ref[4 + k] = dot_nt(out, up_ref[...])
        wide_ref[:, k * RANK:(k + 1) * RANK] = act
        cross = dot(in_ref[k], up_ref[...], (0, 1))
        wide_ref[:, (4 + k) * RANK:(5 + k) * RANK] = cross.astype(BF)
        at = 8 * RANK + k * span
        wide_ref[:, at:at + span] = normed_buf[:, own]
        at += 4 * span
        wide_ref[:, at:at + span] = out_buf[k, :, own]
        in_window_ref[k * span:(k + 1) * span, :] = in_ref[k, own, :]
    scale = lax.rsqrt(total * (1.0 / (4 * width)) + EPS)
    proj = jnp.zeros((RANK, RANK), F32)
    for k in range(4):
        proj = proj + dot_nn((out_buf[k].astype(F32) * scale).astype(BF), in_ref[k])
    state_ref[8] = proj
    pre_ref[...] = proj
    state_ref[9] = jnp.broadcast_to(scale, (RANK, RANK))
    per = sections // 4
    own = pl.ds(
        pl.multiple_of(lax.rem(sec, per) * in_windows[0], RANK), in_windows[1] * RANK
    )
    out = out_buf[sec // per, :, own].astype(F32)
    wide_ref[:, 8 * RANK + 8 * span:] = (out * scale).astype(BF)


def encoder_front(sec, images, enc_down, enc_up, proj_in):
    sections = images.shape[0]
    width = images.shape[3]
    windows = window(width, sections)
    in_windows = window(width, sections // 4)
    span = windows[1] * RANK
    total = 8 * RANK + 8 * span + in_windows[1] * RANK
    return pl.pallas_call(
        functools.partial(front_kernel, sections, windows, in_windows),
        in_specs=[SMEM] + [VMEM] * 4,
        out_specs=[VMEM] * 4,
        out_shape=[
            jax.ShapeDtypeStruct((10, RANK, RANK), F32),
            jax.ShapeDtypeStruct((RANK, RANK), F32),
            jax.ShapeDtypeStruct((RANK, total), BF),
            jax.ShapeDtypeStruct((4 * span, RANK), BF),
        ],
        scratch_shapes=[
            pltpu.VMEM((RANK, width), BF),
            pltpu.VMEM((4, RANK, width), BF),
        ],
        compiler_params=PARAMS,
    )(scalars(sec), images, enc_down, enc_up, proj_in)


def pack_kernel(layers, core_ref, gram_ref, out_ref, packed):
    at = 0
    for l in range(layers):
        size = (l + 2) * 16
        packed[at:at + size, :] = gram_ref[l, :size, :]
        at += size
    half = at // 2
    value = packed[pl.ds(pl.multiple_of(core_ref[0] * half, 16), half), :]
    for to in range(out_ref.shape[0]):
        out_ref[to] = value


def pack_gram(core, gram, groups):
    layers = gram.shape[0]
    total = sum((l + 2) * 16 for l in range(layers))
    return pl.pallas_call(
        functools.partial(pack_kernel, layers),
        in_specs=[SMEM, VMEM],
        out_specs=VMEM,
        out_shape=jax.ShapeDtypeStruct((groups, total // 2, RANK), BF),
        scratch_shapes=[pltpu.VMEM((total, RANK), BF)],
        compiler_params=PARAMS,
    )(scalars(core), gram)


def rank_kernel(
    layers, width,
    place_ref, own_ref, other_ref, gath_ref, proj_pre_ref, base_ref, sel_ref,
    coef_ref, factor_ref, image_ref,
    weight, acts, act_cat, grads, scaled, back, pre_ref, slope_ref, inner_ref, scale_ref,
):
    rank = RANK
    own = place_ref[0]
    core = place_ref[1]
    at = 0
    for l in range(layers):
        for j in range(l + 2):
            which, place = divmod(at, own_ref.shape[1])
            span = slice(place, place + 16)
            tile = jnp.where(core == which, own_ref[:, span, :], other_ref[:, span, :])
            tile = tile.astype(F32)
            rows = slice(j * rank, (j + 1) * rank)
            weight[l, rows, :rank] = tile[:, :8, :].reshape(rank, rank).astype(BF)
            weight[l, rows, rank:] = tile[:, 8:, :].reshape(rank, rank).astype(BF)
            at += 16

    proj_pre = proj_pre_ref[...]
    sel = sel_ref[...]
    placed = dot_nn(sel, gelu_tanh(proj_pre).astype(BF))
    placed_half = placed.astype(BF)
    acts[0] = placed_half
    act_cat[:, :rank] = placed_half
    image_inner = dot_nn(placed_half, base_ref[1].astype(BF))
    total = base_ref[2][:, :1] + jnp.sum(placed * image_inner, axis=1, keepdims=True)
    for l in range(layers):
        here = (l + 1) * rank
        scale = lax.rsqrt(jnp.maximum(total, 0.0) * (1.0 / width) + EPS)
        both = dot_nn(act_cat[:, :here], weight[l, :here, :])
        pre = scale * (gath_ref[l, :rank, :].astype(F32) + both[:, :rank])
        inner = gath_ref[l, rank:2 * rank, :].astype(F32) + both[:, rank:]
        sig = jax.nn.sigmoid(pre)
        act = (pre * sig).astype(BF)
        acts[l + 1] = act
        act_cat[:, here:here + rank] = act
        after = inner + dot_nn(act, weight[l, here:here + rank, rank:])
        total = total + jnp.sum(act.astype(F32) * (inner + after), axis=1, keepdims=True)
        pre_ref[l] = pre
        slope_ref[l] = sig * (1.0 + pre * (1.0 - sig))
        inner_ref[l] = after
        scale_ref[l] = scale
    back[...] = jnp.zeros_like(back)
    sums = jnp.zeros_like(total)
    for l in reversed(range(layers)):
        here = (l + 1) * rank
        cot = gath_ref[l, 2 * rank:3 * rank, :].astype(F32)
        d_act = cot - sums * inner_ref[l] + back[:, here:here + rank]
        d_pre = (d_act * slope_ref[l]).astype(BF).astype(F32)
        scale = scale_ref[l]
        mean = jnp.sum(d_pre * pre_ref[l], axis=1, keepdims=True) * (1.0 / width)
        grad = (scale * d_pre).astype(BF)
        part = (sums * acts[l + 1].astype(F32)).astype(BF)
        grads[l] = grad
        scaled[l + 1] = part
        pair = jnp.concatenate([grad, -part], axis=1)
        back[:, :here] += dot_nt(pair, weight[l, :here, :])
        sums = sums + scale * scale * mean
    d_image = base_ref[0] - sums * image_inner + back[:, :rank]
    scaled[0] = (sums * placed).astype(BF)
    d_slot = dot_tn(sel, d_image.astype(BF))
    image_ref[0] = (d_slot * gelu_slope(proj_pre)).astype(BF)
    image_ref[1] = placed_half
    image_ref[2] = scaled[0]

    own_act = acts[own + 1]
    own_grad = grads[own]
    own_scaled = scaled[own + 1]
    factor_ref[0] = own_grad
    factor_ref[1] = own_act
    factor_ref[2] = own_scaled
    coef_ref[0] = dot_tn(acts[0], own_grad).astype(BF)
    for l in range(layers):
        low = l < own
        left = jnp.where(low, acts[l + 1], grads[l])
        right = jnp.where(low, own_grad, own_act)
        coef_ref[l + 1] = dot_tn(left, right).astype(BF)
    for l in range(layers + 1):
        low = l <= own + 1
        left = jnp.where(low, acts[l], scaled[l])
        right = jnp.where(low, own_scaled, own_act)
        coef_ref[layers + 1 + l] = dot_tn(left, right).astype(BF)


def rank_space(position, core, gram, other, gath, proj_pre, base, sel, width):
    layers = gath.shape[0]
    rank = RANK
    tall = (layers + 1) * rank
    operands = (gram, other, gath, proj_pre, base, sel)

    def whole(shape):
        return pl.BlockSpec(shape, lambda i: (0,) * len(shape))

    outs = ((2 * layers + 2, rank, rank), (3, rank, rank), (3, rank, rank))
    return pl.pallas_call(
        functools.partial(rank_kernel, layers, width),
        grid=(1,),
        in_specs=[SMEM] + [whole(value.shape) for value in operands],
        out_specs=[whole(shape) for shape in outs],
        out_shape=[jax.ShapeDtypeStruct(shape, BF) for shape in outs],
        scratch_shapes=[
            pltpu.VMEM((layers, tall, 2 * rank), BF),
            pltpu.VMEM((layers + 1, rank, rank), BF),
            pltpu.VMEM((rank, tall), BF),
            pltpu.VMEM((layers, rank, rank), BF),
            pltpu.VMEM((layers + 1, rank, rank), BF),
            pltpu.VMEM((rank, tall), F32),
            pltpu.VMEM((layers, rank, rank), F32),
            pltpu.VMEM((layers, rank, rank), F32),
            pltpu.VMEM((layers, rank, rank), F32),
            pltpu.VMEM((layers, rank, 1), F32),
        ],
        compiler_params=pltpu.CompilerParams(vmem_limit_bytes=60 * 1024 * 1024),
    )(scalars(position, core), *operands)


def late_kernel(
    enc_width, tiles, in_tiles, pieces,
    shift_ref, image_ref, state_ref, wide_ref, in_ref, block_ref,
    part_ref,
    down, up, proj, last,
):
    span = tiles * RANK
    d_proj = image_ref[0]
    placed = image_ref[1]
    d_proj32 = d_proj.astype(F32)
    proj_scale = state_ref[9]
    mean = jnp.sum(d_proj32 * state_ref[8], axis=1, keepdims=True) * (1.0 / (4 * enc_width))
    d_scaled = (d_proj32 * proj_scale).astype(BF)
    pull = mean * proj_scale * proj_scale
    total_down = jnp.zeros((span, RANK), F32)
    total_up = jnp.zeros((span, RANK), F32)
    for k in range(4):
        act = wide_ref[:, k * RANK:(k + 1) * RANK]
        cross = wide_ref[:, (4 + k) * RANK:(5 + k) * RANK]
        at = 8 * RANK + k * span
        normed = wide_ref[:, at:at + span]
        at += 4 * span
        out = wide_ref[:, at:at + span]
        d_enc = (dot_nn(d_scaled, cross) - pull * state_ref[4 + k]) * state_ref[k]
        total_down += dot_tn(normed, d_enc.astype(BF))
        inner = dot_tn(d_scaled, act).astype(BF)
        total_up += dot_nn(in_ref[k * span:(k + 1) * span, :], inner)
        total_up -= dot_tn(out, (pull * act.astype(F32)).astype(BF))
    down[:span, :] = total_down
    up[:span, :] = total_up
    proj[:in_tiles * RANK, :] = dot_tn(wide_ref[:, 8 * RANK + 8 * span:], d_proj)
    last[...] = dot_tn(block_ref[0], placed) - dot_tn(
        block_ref[1], dot_tn(placed, image_ref[2]).astype(BF)
    )
    groups = part_ref.shape[0]
    n_enc, n_in, pad_enc, pad_in = pieces
    n_out = last.shape[0] // groups
    for to in range(groups):
        at = shift_ref[0] + n_enc * to
        part_ref[to, :pad_enc, :] = down[pl.ds(at, pad_enc), :].astype(BF)
        part_ref[to, pad_enc:2 * pad_enc, :] = up[pl.ds(at, pad_enc), :].astype(BF)
        at = shift_ref[1] + n_in * to
        part_ref[to, 2 * pad_enc:2 * pad_enc + pad_in, :] = proj[pl.ds(at, pad_in), :].astype(BF)
        part_ref[to, 2 * pad_enc + pad_in:, :] = last[to * n_out:(to + 1) * n_out, :].astype(BF)


def encoder_late(sec, image, state, wide, in_window, blocks, enc_width, sections, groups):
    tiles = window(enc_width, sections)[1]
    in_tiles = window(enc_width, sections // 4)[1]
    block = enc_width // sections
    in_block = 4 * block
    n_enc = block // groups
    n_in = in_block // groups
    pad_enc = -(-n_enc // 16) * 16
    pad_in = -(-n_in // 16) * 16
    shifts = scalars(
        sec * (block % RANK), (sec % (sections // 4)) * (in_block % RANK)
    )
    columns = blocks.shape[2]
    total = 2 * pad_enc + pad_in + columns // groups
    pieces = (n_enc, n_in, pad_enc, pad_in)
    parts = pl.pallas_call(
        functools.partial(late_kernel, enc_width, tiles, in_tiles, pieces),
        in_specs=[SMEM] + [VMEM] * 5,
        out_specs=VMEM,
        out_shape=jax.ShapeDtypeStruct((groups, total, RANK), BF),
        scratch_shapes=[
            pltpu.VMEM((tiles * RANK + 16, RANK), F32),
            pltpu.VMEM((tiles * RANK + 16, RANK), F32),
            pltpu.VMEM((in_tiles * RANK + 16, RANK), F32),
            pltpu.VMEM((columns, RANK), F32),
        ],
        compiler_params=PARAMS,
    )(shifts, image, state, wide, in_window, blocks)
    return parts, pieces


def row_kernel(
    place_ref, first_ref, second_ref, third_ref, fourth_ref, factor_ref,
    down_ref, up_ref,
):
    groups, rows, share = first_ref.shape
    part = rows // 2

    def flat(value):
        return value.reshape(groups * part, value.shape[-1])

    total_down = jnp.zeros((share, RANK), F32)
    total_up = jnp.zeros((RANK, share), F32)
    own = place_ref[0]
    for at, cols_ref in enumerate((first_ref, second_ref, third_ref, fourth_ref)):
        which = lax.rem(own, 2) if at % 2 == 0 else 1 - lax.rem(own, 2)
        which = which + 2 * (own // 2 if at < 2 else 1 - own // 2)
        start = pl.multiple_of(which * part, part)
        text = flat(cols_ref[:, :part, :])
        cot = flat(cols_ref[:, part:, :])
        span = pl.ds(start, part)
        total_down += dot_tn(text, flat(factor_ref[:, 0, span, :]))
        total_up += dot_tn(flat(factor_ref[:, 1, span, :]), cot)
        total_up -= dot_tn(flat(factor_ref[:, 2, span, :]), text)
    down_ref[...] = total_down
    up_ref[...] = total_up


def row_products(sec, cols, factors):
    share = cols[0].shape[2]
    return pl.pallas_call(
        row_kernel,
        in_specs=[SMEM] + [VMEM] * 5,
        out_specs=[VMEM] * 2,
        out_shape=[
            jax.ShapeDtypeStruct((share, RANK), F32),
            jax.ShapeDtypeStruct((RANK, share), F32),
        ],
        compiler_params=PARAMS,
    )(scalars(sec % 4), *cols, factors)


def last_kernel(
    layers,
    place_ref, down_ref, up_ref, mixed_ref, slice_ref, out_ref,
    grad_down_ref, grad_up_ref,
    coef,
):
    sec = place_ref[0]
    groups = mixed_ref.shape[0]
    share = out_ref.shape[1]
    chunk = coef.shape[0] // groups
    for at in range(groups):
        coef[at * chunk:(at + 1) * chunk, :] = mixed_ref[at, :chunk, :]

    def block(index):
        return coef[index * RANK:(index + 1) * RANK, :]

    total_down = down_ref[...] + dot_tn(out_ref[...], block(0))
    total_up = up_ref[...] - dot_tn(block(layers + 1), out_ref[...])
    turned = jnp.zeros((share, RANK), F32)
    for l in range(layers):
        pair = block(l + 1)
        zero = jnp.zeros_like(pair)
        up = jnp.concatenate(
            [
                slice_ref[l, share + m * RANK:share + (m + 1) * RANK, :]
                for m in range(share // RANK)
            ],
            axis=1,
        )
        total_down += dot_tn(up, jnp.where(l < sec, pair, zero))
        turned += dot_nn(slice_ref[l, :share, :], jnp.where(l > sec, pair, zero))
        total_up -= dot_tn(block(layers + 2 + l), up)
    grad_down_ref[...] = total_down
    grad_up_ref[...] = total_up + turned.T


def last_products(sec, down, up, mixed, slices, out):
    layers = slices.shape[0]
    share = out.shape[1]
    return pl.pallas_call(
        functools.partial(last_kernel, layers),
        in_specs=[SMEM] + [VMEM] * 5,
        out_specs=[VMEM] * 2,
        out_shape=[
            jax.ShapeDtypeStruct((share, RANK), F32),
            jax.ShapeDtypeStruct((RANK, share), F32),
        ],
        scratch_shapes=[pltpu.VMEM(((2 * layers + 2) * RANK, RANK), BF)],
        compiler_params=PARAMS,
    )(scalars(sec), down, up, mixed, slices, out)


def spread(value, axis):
    count = lax.axis_size(axis)
    return lax.all_to_all(jnp.broadcast_to(value[None], (count,) + value.shape), axis, 0, 0)


def shards(text, cotangent, dec_down, dec_up, images, enc_down, enc_up, proj_in, proj_out, frame):
    sections = lax.axis_size("section")
    groups = lax.axis_size("dp")
    sec = lax.axis_index("section")
    grp = lax.axis_index("dp")
    core = sec % 2
    slot_count, patch_count, enc_width = images.shape[2:]
    tokens = patch_count // 4
    rows_total, width = text.shape[1:]
    rank = dec_down.shape[2]
    weight_down = dec_down[0]
    weight_up = dec_up[0]
    frames = frame[0]
    text = text[0]
    cot = cotangent[0]
    piece = rank // groups
    swap = [(at, at ^ 1) for at in range(sections)]

    own_rows = lax.dynamic_slice_in_dim(weight_up, grp * piece, piece, 0)
    own_rows, frames = lax.optimization_barrier((own_rows, frames))
    up_rows = spread(own_rows, "section")

    slot_row = jnp.repeat(frames, tokens)[None, :]
    row = jnp.arange(rows_total, dtype=jnp.int32)[:, None]
    column = jnp.arange(rows_total, dtype=jnp.int32)[None, :]
    sel = (slot_row == row // tokens) & (row % tokens == column % tokens)
    keep = 1.0 - jnp.any(sel, axis=1, keepdims=True).astype(F32)
    sel = sel.astype(BF)
    cols, proj, base, picks, blocks, own_slices, out_slice = (
        text_products(
            sec, grp, keep, text, cot, weight_down, weight_up, proj_out, sections, groups
        )
    )
    own_images = images[0, 0].reshape(slot_count * tokens, 4, enc_width).transpose(1, 0, 2)

    image_rows = lax.dynamic_slice_in_dim(proj_out, grp * piece, piece, 0)
    up_rows, cols, own_images, image_rows = lax.optimization_barrier(
        (up_rows, cols, own_images, image_rows)
    )
    cols = lax.all_to_all(cols, "dp", 0, 0)
    group_images = lax.all_gather(own_images, "section", axis=0)
    rows = jnp.concatenate([image_rows[None], up_rows], axis=0).reshape(-1, width)
    gram = jnp.stack(
        [
            dot_nn(rows, weight_down).reshape(sections + 1, piece, rank),
            dot_nt(rows, weight_up).reshape(sections + 1, piece, rank),
        ],
        axis=1,
    ).astype(BF).reshape(-1, rank)
    packed = pack_gram(core, lax.all_gather(gram, "section", axis=0), groups)
    packed, cols, proj = lax.optimization_barrier((packed, cols, proj))
    own_gram = lax.all_to_all(packed, "dp", 0, 0)

    gath = lax.all_gather(proj, "section", axis=0)
    quarters = proj_in.reshape(4, enc_width, rank)
    state, proj_pre, wide, in_window = encoder_front(
        sec, group_images, enc_down, enc_up, quarters
    )
    own_gram, gath, state, proj_pre, wide, in_window, cols, own_slices = lax.optimization_barrier(
        (own_gram, gath, state, proj_pre, wide, in_window, cols, own_slices)
    )
    slices = lax.all_gather(own_slices, "section", axis=0)
    other_gram = lax.ppermute(own_gram, "section", swap)
    far = [(at, at ^ 2) for at in range(sections)]
    far_cols = lax.ppermute(cols, "section", far)

    coef, factor, image = rank_space(
        sec, core, own_gram, other_gram, gath, proj_pre, base, sel, width
    )
    coef = lax.all_to_all(coef.reshape(groups, -1, rank), "dp", 0, 0)
    factors = lax.all_gather(factor, "dp", axis=0)

    parts, (n_enc, n_in, pad_enc, pad_in) = encoder_late(
        sec, image, state, wide, in_window, blocks, enc_width, sections, groups
    )
    coef = jnp.sum(coef.astype(F32), axis=0).astype(BF)
    coef, far_cols = lax.optimization_barrier((coef, far_cols))
    chunk = coef.shape[0]
    mixed = jnp.concatenate(
        [jnp.broadcast_to(coef[None], (groups,) + coef.shape), parts], axis=1
    )
    mixed = lax.all_to_all(mixed, "dp", 0, 0)

    first_coef = mixed[0, :rank]
    at = (sections + 1) * rank
    last_coef = mixed[at // chunk, at % chunk:at % chunk + rank]
    few = picks.shape[2]
    term = dot_nt(picks[:, 0].reshape(-1, rank), first_coef)
    term = term - dot_nt(picks[:, 1].reshape(-1, rank), last_coef)
    term = lax.all_to_all(term.astype(BF).reshape(sections, few, rank), "section", 0, 0)

    every_cols = (
        cols, lax.ppermute(cols, "section", swap),
        far_cols, lax.ppermute(far_cols, "section", swap),
    )
    row_down, row_up = row_products(sec, every_cols, factors)
    grad_dec_down, grad_dec_up = last_products(
        sec, row_down, row_up, mixed, slices, out_slice
    )
    parts = jnp.sum(mixed[:, chunk:].astype(F32), axis=0)
    grad_enc_down = parts[:n_enc]
    grad_enc_up = parts[pad_enc:pad_enc + n_enc].T
    grad_proj_in = parts[2 * pad_enc:2 * pad_enc + n_in]
    own_out = parts[2 * pad_enc + pad_in:]
    grad_proj_out = (own_out + jnp.sum(term.astype(F32), axis=0)).T
    return (
        grad_dec_down[None],
        grad_dec_up[None],
        grad_enc_down,
        grad_enc_up,
        grad_proj_in,
        grad_proj_out,
    )


def solution(mesh):
    placed = (
        P("dp", None, None),
        P("dp", None, None),
        P("section", None, None),
        P("section", None, None),
        P("dp", "section", None, None, None),
        P(),
        P(),
        P(),
        P(),
        P("dp", None),
    )
    return jax.shard_map(
        shards,
        mesh=mesh,
        in_specs=placed,
        out_specs=(
            P("section", "dp", None),
            P("section", None, "dp"),
            P(("section", "dp"), None),
            P(None, ("section", "dp")),
            P(("section", "dp"), None),
            P(None, ("section", "dp")),
        ),
        check_vma=False,
    )
```
